256 devices in a mesh: dp: 32 (over y_hi, z, core), layer: 8 (over y_lo, x).
Axes of the slice: x: 4, y: 4 (y_hi: 2, y_lo: 2; y = y_hi * 2 + y_lo), z: 8, core: 2. Of those that a mesh axis runs over, the one named last changes fastest.
Arguments:
- activations: bfloat16 [8, 8192, 5120], P('layer', 'dp'), may hold values from -6 to 6
- backprops: bfloat16 [8, 8192, 5120], P('layer', 'dp'), may hold values from -6 to 6
- out_factors: bfloat16 [8, 32, 32, 5120], P('layer', 'dp'), may hold values from -0.078125 to 0.078125
- in_factors: bfloat16 [8, 32, 32, 5120], P('layer', 'dp'), may hold values from -0.078125 to 0.078125
- doc_lengths: int32 [32, 4], P('dp'), may hold values from 1 to 128, 256 in all within a row
Outputs:
- scores: float32 [32, 128], P('layer', 'dp')
The draws below stay inside these ranges and needn't reach their ends.
Inputs may be any that keep to these rules, and one draw needn't show every extreme that they name: `doc_lengths`: each row holds the lengths of 4 documents that sum to 256; every row has one of length 128.
All inputs are finite; a program needn't handle non-finite values.
Results may differ from the reference program's by a relative error of at most 0.0003.
Values may be sent and summed in bfloat16 or wider, within the bound.
A program may use at most 128 MiB of HBM per device.

```python
import math
import jax
import jax.numpy as jnp
import numpy as np
from jax import lax

D = 5120
RANK = 32
TOK_DEV = 256
DOCS_DEV = 4
MOST = 128
LAYERS = 8
QUERIES = 32
TOKENS = 8192
DOCUMENTS = 128
SHARDS = 32


def level_of(rng, shape, split, least, largest):
    loudness, own = 1.0, jax.random.fold_in(rng, 6)
    for dim, blocks in split:
        steps = jnp.exp(jax.random.uniform(jax.random.fold_in(own, dim), (blocks,), jnp.float32, least / len(split), largest / len(split)))
        loudness = loudness * jnp.repeat(steps, shape[dim] // blocks).reshape([-1 if axis == dim else 1 for axis in range(len(shape))])
    return loudness


def profile(number_of, total, reach, lean):
    portions = [(1 << 20) // math.isqrt(rank ** lean) + 1 for rank in range(2, number_of + 1)]
    spare, counts = total - reach - (number_of - 1), [1] * (number_of - 1)
    while spare > 0:
        free = [i for i in range(number_of - 1) if counts[i] < reach]
        pool, budget = sum([portions[i] for i in free]), spare
        for i in free:
            extra = min(reach - counts[i], max(1, budget * portions[i] // pool), spare)
            counts[i] = counts[i] + extra
            spare = spare - extra
    return np.array([reach] + counts)


def uneven(stream_key, count, total, bound, slope):
    if count == 2:
        one = jax.random.randint(stream_key, (), max(1, total - bound), min(bound, total - 1) + 1)
        return jnp.stack([one, total - one])
    tallies = jnp.asarray(profile(count, total, bound, slope), jnp.int32)
    couples = (count - 1) // 2
    donor, sink = tallies[1:1 + 2 * couples:2], tallies[2:2 + 2 * couples:2]
    room = jnp.minimum(donor - 1, bound - sink)
    moved = jax.random.randint(jax.random.fold_in(stream_key, 1), (couples,), 0, 1 << 20) % (room + 1)
    tallies = tallies.at[1:1 + 2 * couples:2].set(donor - moved).at[2:2 + 2 * couples:2].set(sink + moved)
    return tallies[jax.random.permutation(jax.random.fold_in(stream_key, 2), count)]


def scatter_about(stream_key, dims, spread, reach, cuts=(), dtype=jnp.bfloat16):
    level = level_of(stream_key, dims, cuts, -0.22, 0.18) if cuts else 1.0
    values = jax.random.normal(stream_key, dims, jnp.float32) * spread * level
    return jnp.minimum(jnp.maximum(values, -reach), reach).astype(dtype)


def setup_inputs(seed: int = 0) -> dict:
    streams_of = jax.random.split(jax.random.key(seed), 6)
    return {
        "activations": scatter_about(streams_of[0], (LAYERS, TOKENS, D), 1.0, 6.0, ((0, 8), (1, 32))),
        "backprops": scatter_about(streams_of[1], (LAYERS, TOKENS, D), 1.0, 6.0, ((0, 8), (1, 32))),
        "out_factors": scatter_about(streams_of[2], (LAYERS, QUERIES, RANK, D), D ** -0.5, 0.078125, ((0, 8), (1, 32))),
        "in_factors": scatter_about(streams_of[3], (LAYERS, QUERIES, RANK, D), D ** -0.5, 0.078125, ((0, 8), (1, 32))),
        "doc_lengths": jax.vmap(lambda own: uneven(own, DOCS_DEV, TOK_DEV, MOST, 1))(jax.random.split(streams_of[4], SHARDS)).reshape((SHARDS, DOCS_DEV)).astype(jnp.int32),
    }


def doc_members(doc_lengths):
    doc_ends = jnp.cumsum(doc_lengths, axis=1).astype(jnp.int32)
    doc_starts = doc_ends - doc_lengths
    position = lax.iota(jnp.int32, TOK_DEV)
    inside = (position[None, None, :] >= doc_starts[:, :, None]) & (position[None, None, :] < doc_ends[:, :, None])
    return inside.astype(jnp.float32)

def reference(activations, backprops, out_factors, in_factors, doc_lengths):
    member = doc_members(doc_lengths)

    def one_layer(running, layer_inputs):
        acts, grads, outs_layer, ins_layer = layer_inputs
        out_proj = lax.dot_general(grads, outs_layer.reshape(QUERIES * RANK, D), (((1,), (1,)), ((), ())), preferred_element_type=jnp.float32)
        in_proj = lax.dot_general(acts, ins_layer.reshape(QUERIES * RANK, D), (((1,), (1,)), ((), ())), preferred_element_type=jnp.float32)
        token_terms = (out_proj * in_proj).reshape(TOKENS, QUERIES, RANK).sum(axis=-1)
        shard_terms = token_terms.reshape(SHARDS, TOK_DEV, QUERIES)
        layer_scores = jnp.einsum('skt,stq->qsk', member, shard_terms, precision=lax.Precision.HIGHEST)
        return (running + layer_scores.reshape(QUERIES, DOCUMENTS), None)
    start_tile = jnp.zeros((QUERIES, DOCUMENTS), jnp.float32)
    summed, _ = lax.scan(one_layer, start_tile, (activations, backprops, out_factors, in_factors))
    scaling = 1.0 / math.sqrt(RANK * LAYERS * TOK_DEV / DOCS_DEV)
    return summed * scaling
```

```python
import functools
import math

import jax
import jax.numpy as jnp
from jax import lax
from jax.experimental import pallas as pl
from jax.experimental.pallas import tpu as pltpu
from jax.sharding import PartitionSpec as P

MESH = pl.DeviceIdType.MESH
RING = 8
LINES = 2
CORES = 2
CHUNKS = 8

SENDS = (
    ("p1", 1, 0, 0, 0, 2, 0),
    ("m1", -1, 0, 0, 0, 2, 0),
    ("y1", 0, 0, 0, 0, 2, 0),
    ("p2", 1, 0, -1, 0, 2, 1),
    ("m2", -1, 0, 1, 0, 2, 1),
    ("p5", 1, 1, 0, 0, 2, 1),
    ("m5", -1, 1, 0, 0, 2, 1),
    ("p3", 1, 0, -2, 0, 2, 2),
    ("y2", 0, 0, -2, 0, 2, 2),
    ("m3", -1, 0, 2, 0, 2, 2),
    ("y3", 0, 0, 2, 0, 2, 2),
    ("p4", 1, 0, -3, 0, 1, 3),
    ("y4", 0, 0, -3, 0, 2, 3),
    ("m4", -1, 0, 3, 1, 1, 3),
    ("y5", 0, 0, 3, 0, 2, 3),
    ("p6", 1, 1, -3, 0, 1, 4),
    ("m6", -1, 1, 3, 1, 1, 4),
)
NEEDS = {
    "p2": "p1", "m2": "m1", "p5": "y1", "p3": "p2", "m3": "m2",
    "p4": "p3", "m4": "m3", "p6": "y4", "m6": "y5",
}
LAST = ("p5", "m5", "y2", "y3", "p4", "m4", "p6", "m6")
LAST_LAG = 5
INDEX = {send[0]: i for i, send in enumerate(SENDS)}


def kernel(
    layers, lens_ref, acts_ref, grads_ref, outs_ref, ins_ref, result_ref,
    gathered, tokens, proj, member, tiles, landed,
    own_sem, tok_sem, tok_send, tok_recv, send_sem, recv_sem, mem_send, mem_recv, tile_send, tile_recv,
):
    dp, layer = lax.axis_index("dp"), lax.axis_index("layer")
    line, ring, core = dp // (RING * CORES), (dp // CORES) % RING, dp % CORES
    rank, width = outs_ref.shape[2], outs_ref.shape[3]
    count = acts_ref.shape[1]
    docs = lens_ref.shape[1]
    columns = width // CHUNKS

    def device(line_, ring_, core_):
        return (line_ * RING + ring_) * CORES + core_

    up = (device(line, (ring + 1) % RING, core), layer)
    down = (device(line, (ring + RING - 1) % RING, core), layer)
    across = (device(1 - line, ring, core), layer)
    sibling = (device(line, ring, 1 - core), layer)
    hop = {1: up, -1: down, 0: across}

    mine = pl.multiple_of((line * RING + ring) * rank, rank)
    half = pl.multiple_of(core * count, count)
    own = [
        pltpu.make_async_copy(f.at[0, 0], gathered.at[i, pl.ds(mine, rank)], own_sem.at[i])
        for i, f in enumerate((outs_ref, ins_ref))
    ]
    here = [
        pltpu.make_async_copy(t.at[0], tokens.at[i, pl.ds(half, count)], tok_sem.at[i])
        for i, t in enumerate((grads_ref, acts_ref))
    ]
    for copy in own + here:
        copy.start()

    barrier = pltpu.get_barrier_semaphore()
    for target in (up, down, across):
        pl.semaphore_signal(barrier, inc=1, device_id=target, device_id_type=MESH)
    for step in range(1, layers * CORES):
        to = (layer * CORES + core + step) % (layers * CORES)
        pl.semaphore_signal(
            barrier, inc=1, device_id=(device(line, ring, to % CORES), to // CORES), device_id_type=MESH
        )

    position = lax.broadcasted_iota(jnp.int32, (8, count), 1)
    row = lax.broadcasted_iota(jnp.int32, (8, count), 0)
    held = jnp.zeros((8, count), jnp.float32)
    first = jnp.int32(0)
    for d in range(docs):
        after = first + lens_ref[0, d]
        inside = (row == core * docs + d) & (position >= first) & (position < after)
        held = jnp.where(inside, 1.0, held)
        first = after
    member[core] = held
    proj[...] = jnp.zeros_like(proj)
    for copy in own:
        copy.wait()
    pl.semaphore_wait(barrier, 3 + layers * CORES - 1)

    def block(name, n, arriving=False):
        _, way, other, offset, part, parts, _ = SENDS[INDEX[name]]
        line_ = line if other == 0 else 1 - line
        if arriving:
            line_ = 1 - line_ if way == 0 else line_
            offset = offset - way
        slot = line_ * RING + (ring + offset + RING) % RING
        rows = pl.ds(pl.multiple_of(slot * rank, rank), rank)
        cols = pl.ds(pl.multiple_of(n * columns, columns), columns)
        return gathered.at[pl.ds(part, parts), rows, cols]

    def transfer(name, n, arriving=False):
        i = INDEX[name]
        ref = block(name, n, arriving)
        return pltpu.make_async_remote_copy(
            src_ref=ref, dst_ref=ref, send_sem=send_sem.at[i, n], recv_sem=recv_sem.at[i, n],
            device_id=hop[SENDS[i][1]], device_id_type=MESH,
        )

    def sends(lag):
        return [s[0] for s in SENDS if s[6] == lag]

    shared = [
        pltpu.make_async_remote_copy(
            src_ref=t.at[0], dst_ref=tokens.at[i, pl.ds(half, count)],
            send_sem=tok_send.at[i], recv_sem=tok_recv.at[i], device_id=sibling, device_id_type=MESH,
        )
        for i, t in enumerate((grads_ref, acts_ref))
    ]
    theirs = pltpu.make_async_remote_copy(
        src_ref=member.at[core], dst_ref=member.at[core],
        send_sem=mem_send, recv_sem=mem_recv, device_id=sibling, device_id_type=MESH,
    )

    def multiply(n):
        cols = pl.ds(pl.multiple_of(n * columns, columns), columns)

        def tile(step, carry):
            i, t = step // CORES, step % CORES
            some = pl.ds(pl.multiple_of(t * count, count), count)
            proj[i, :, some] += lax.dot_general(
                gathered[i, :, cols], tokens[i, some, cols], (((1,), (1,)), ((), ())),
                preferred_element_type=jnp.float32,
            )
            return carry

        lax.fori_loop(0, 2 * CORES, tile, 0)

    def round_of(n, carry):
        for lag in range(LAST_LAG):
            now = n - lag

            @pl.when((now >= 0) & (now < CHUNKS))
            def _():
                for name in sends(lag):
                    if name in NEEDS:
                        transfer(NEEDS[name], now, True).wait_recv()
                    transfer(name, now).start()

            if lag == 0:

                @pl.when(n == 0)
                def _():
                    for copy in shared:
                        copy.start()
                    theirs.start()

        done = n - LAST_LAG

        @pl.when(done == 0)
        def _():
            for i, copy in enumerate(here):
                copy.wait()
            other = pl.ds(pl.multiple_of((1 - core) * count, count), count)
            for i, t in enumerate((grads_ref, acts_ref)):
                pltpu.make_async_remote_copy(
                    src_ref=t.at[0], dst_ref=tokens.at[i, other],
                    send_sem=tok_send.at[i], recv_sem=tok_recv.at[i], device_id=sibling, device_id_type=MESH,
                ).wait_recv()

        @pl.when(done >= 0)
        def _():
            for name in LAST:
                transfer(name, done, True).wait_recv()
            multiply(done)

        return carry

    lax.fori_loop(0, CHUNKS + LAST_LAG, round_of, 0)

    pltpu.make_async_remote_copy(
        src_ref=member.at[1 - core], dst_ref=member.at[1 - core],
        send_sem=mem_send, recv_sem=mem_recv, device_id=sibling, device_id_type=MESH,
    ).wait_recv()
    queries = LINES * RING
    terms = (proj[0] * proj[1]).reshape(queries, rank, CORES * count).sum(axis=1)
    scores = sum(
        lax.dot_general(
            terms[:, t * count : (t + 1) * count], member[t], (((1,), (1,)), ((), ())),
            precision=lax.Precision.HIGHEST, preferred_element_type=jnp.float32,
        )
        for t in range(CORES)
    )
    each = queries // layers
    tile_row = lax.broadcasted_iota(jnp.int32, (8, scores.shape[1]), 0)
    tiles[...] = jnp.zeros_like(tiles)
    for to in range(layers):
        tile = jnp.zeros((8, scores.shape[1]), jnp.float32)
        for i in range(each):
            tile = jnp.where(tile_row == CORES * i + core, scores[to * each + i][None, :], tile)
        tiles[to, :, 0 : scores.shape[1]] = tile

    me = layer * CORES + core
    moves = []
    for step in range(1, layers * CORES):
        to = (me + step) % (layers * CORES)
        moves.append(
            pltpu.make_async_remote_copy(
                src_ref=tiles.at[to // CORES], dst_ref=landed.at[step],
                send_sem=tile_send.at[step], recv_sem=tile_recv.at[step],
                device_id=(device(line, ring, to % CORES), to // CORES), device_id_type=MESH,
            )
        )
    for move in moves:
        move.start()

    def drain(n, carry):
        for send in SENDS:
            transfer(send[0], n).wait_send()
        return carry

    lax.fori_loop(0, CHUNKS, drain, 0)
    for copy in shared:
        copy.wait_send()
    theirs.wait_send()
    total = tiles[layer]
    for step in range(1, layers * CORES):
        moves[step - 1].wait_recv()
        total = total + landed[step]
    for move in moves:
        move.wait_send()
    wide = total[0 : CORES * each]
    result_ref[...] = jnp.where(core == 0, wide[:, 0:docs], wide[:, docs : 2 * docs])


def local(activations, backprops, out_factors, in_factors, doc_lengths):
    count, width = activations.shape[1:]
    rank = out_factors.shape[2]
    docs = doc_lengths.shape[1]
    layers = lax.axis_size("layer") * activations.shape[0]
    queries = LINES * RING
    scaling = 1.0 / math.sqrt(rank * layers * count / docs)
    hbm = pl.BlockSpec(memory_space=pl.ANY)
    dma = pltpu.SemaphoreType.DMA
    flops = 2 * 2 * queries * rank * CORES * count * width
    scores = pl.pallas_call(
        functools.partial(kernel, layers),
        out_shape=jax.ShapeDtypeStruct((CORES * queries // layers, docs), jnp.float32),
        in_specs=[pl.BlockSpec(memory_space=pltpu.SMEM), hbm, hbm, hbm, hbm],
        out_specs=pl.BlockSpec(memory_space=pltpu.VMEM),
        scratch_shapes=[
            pltpu.VMEM((2, queries * rank, width), jnp.bfloat16),
            pltpu.VMEM((2, CORES * count, width), jnp.bfloat16),
            pltpu.VMEM((2, queries * rank, CORES * count), jnp.float32),
            pltpu.VMEM((CORES, 8, count), jnp.float32),
            pltpu.VMEM((layers, 8, 128), jnp.float32),
            pltpu.VMEM((layers * CORES, 8, 128), jnp.float32),
            dma((2,)),
            dma((2,)),
            dma((2,)),
            dma((2,)),
            dma((len(SENDS), CHUNKS)),
            dma((len(SENDS), CHUNKS)),
            dma,
            dma,
            dma((layers * CORES,)),
            dma((layers * CORES,)),
        ],
        compiler_params=pltpu.CompilerParams(
            collective_id=0, has_side_effects=True, vmem_limit_bytes=56 * 2**20
        ),
        cost_estimate=pl.CostEstimate(flops=flops, bytes_accessed=12 * 2**20, transcendentals=0),
        name="gather_scores",
    )(doc_lengths, activations, backprops, out_factors, in_factors)
    return scores * scaling


def solution(mesh):
    placed = (
        P("layer", "dp", None),
        P("layer", "dp", None),
        P("layer", "dp", None, None),
        P("layer", "dp", None, None),
        P("dp", None),
    )
    return jax.shard_map(
        local, mesh=mesh, in_specs=placed, out_specs=P("layer", "dp"), check_vma=False
    )
```

```python
import functools
import math

import jax
import jax.numpy as jnp
from jax import lax
from jax.experimental import pallas as pl
from jax.experimental.pallas import tpu as pltpu
from jax.sharding import PartitionSpec as P

MESH = pl.DeviceIdType.MESH
RING = 8
LINES = 2
CORES = 2
SHARE = 6
UNIT = 128
SIZES = (16, 14, 10)

ORDER = (
    (0, 0, 0, 1), (-1, 0, 0, 0), (1, 0, 0, 0), (0, 0, 0, 0), (1, 0, 0, 1), (0, 0, 0, 2),
    (-1, 0, 0, 1), (-1, 0, 1, 0), (1, 0, -1, 0), (0, 0, -1, 1), (1, 0, -1, 1), (1, 0, 0, 2),
    (-1, 0, 1, 1), (-1, 0, 0, 2), (0, 0, -2, 0), (-1, 0, 2, 0), (1, 0, -2, 1), (0, 0, 2, 1),
    (1, 0, -2, 0), (-1, 0, 2, 1), (1, 0, -1, 2), (-1, 0, 1, 2), (0, 0, -2, 1), (0, 0, 2, 0),
    (1, 0, -3, 1), (-1, 1, 2, 1), (-1, 1, 0, 0), (0, 0, 3, 0), (-1, 0, 2, 2), (0, 0, -3, 0),
    (1, 0, -2, 2), (1, 0, -3, 0), (1, 1, -2, 1), (2, 0, 0, 1), (-1, 0, 3, 0), (0, 0, 1, 1),
    (1, 1, 0, 0), (0, 0, -3, 2), (-1, 1, 3, 1), (0, 0, 3, 2), (-1, 1, 3, 0), (1, 0, -3, 2),
    (1, 1, -3, 1), (0, 0, -2, 2), (-1, 0, 3, 1), (2, 0, 0, 0), (1, 1, 0, 2), (0, 0, 2, 2),
    (-1, 0, 3, 2), (2, 0, 0, 2), (1, 1, -3, 0), (1, 1, -3, 2), (-1, 1, 0, 2), (2, 1, 1, 1),
    (2, 1, 1, 0), (-1, 1, 3, 2), (2, 0, 1, 0), (2, 1, 0, 1), (2, 0, 1, 1), (2, 0, 1, 2),
    (2, 1, 0, 0), (2, 1, 1, 2), (2, 1, 0, 2),
)
SENDS = tuple(item for item in ORDER if item[0] != 2)
INDEX = {item: i for i, item in enumerate(SENDS)}


def far(offset):
    return RING // 2 if abs(offset) == RING // 2 else offset


def halves(item):
    way, _, offset, _ = item
    if way and abs(offset - way) == RING // 2:
        return (0,) if way == 1 else (1,)
    return (0, 1)


def arrival(item):
    way, line, offset, _ = item
    return (1 - line, far(offset)) if way == 0 else (line, far(offset - way))


ARRIVES = {(*arrival(item), half, item[3]): item for item in SENDS for half in halves(item)}


def kernel(
    layers, lens_ref, acts_ref, grads_ref, outs_ref, ins_ref, result_ref,
    tokens, proj, member, tiles, landed,
    own_sem, tok_sem, tok_send, tok_recv, send_sem, recv_sem, mem_send, mem_recv, tile_send, tile_recv,
    *gathered,
):
    dp, layer = lax.axis_index("dp"), lax.axis_index("layer")
    line, ring, core = dp // (RING * CORES), (dp // CORES) % RING, dp % CORES
    rank, width = outs_ref.shape[2], outs_ref.shape[3]
    count = acts_ref.shape[1]
    docs = lens_ref.shape[1]
    starts = [UNIT * sum(SIZES[:c]) for c in range(len(SIZES))]
    columns = [pl.ds(start, UNIT * size) for start, size in zip(starts, SIZES)]

    def device(line_, ring_, core_):
        return (line_ * RING + ring_) * CORES + core_

    up = (device(line, (ring + 1) % RING, core), layer)
    down = (device(line, (ring + RING - 1) % RING, core), layer)
    across = (device(1 - line, ring, core), layer)
    sibling = (device(line, ring, 1 - core), layer)
    hop = {1: up, -1: down, 0: across}

    mine = line * RING + ring
    half = pl.multiple_of(core * count, count)
    own = [
        pltpu.make_async_copy(f.at[0, 0, :, columns[c]], gathered[c].at[mine, i], own_sem.at[c, i])
        for c in range(len(SIZES))
        for i, f in enumerate((outs_ref, ins_ref))
    ]
    here = [
        pltpu.make_async_copy(t.at[0], tokens.at[i, pl.ds(half, count)], tok_sem.at[i])
        for i, t in enumerate((grads_ref, acts_ref))
    ]
    for copy in own + here:
        copy.start()

    barrier = pltpu.get_barrier_semaphore()
    for target in (up, down, across):
        pl.semaphore_signal(barrier, inc=1, device_id=target, device_id_type=MESH)
    for step in range(1, layers * CORES):
        to = (layer * CORES + core + step) % (layers * CORES)
        pl.semaphore_signal(
            barrier, inc=1, device_id=(device(line, ring, to % CORES), to // CORES), device_id_type=MESH
        )

    position = lax.broadcasted_iota(jnp.int32, (8, count), 1)
    row = lax.broadcasted_iota(jnp.int32, (8, count), 0)
    held = jnp.zeros((8, count), jnp.float32)
    first = jnp.int32(0)
    for d in range(docs):
        after = first + lens_ref[0, d]
        inside = (row == core * docs + d) & (position >= first) & (position < after)
        held = jnp.where(inside, 1.0, held)
        first = after
    member[core] = held
    for copy in own:
        copy.wait()
    pl.semaphore_wait(barrier, 3 + layers * CORES - 1)

    def block(line_, offset, item):
        part = halves(item)
        slot = (line if line_ == 0 else 1 - line) * RING + (ring + offset + RING) % RING
        return gathered[item[3]].at[slot, pl.ds(part[0], len(part))]

    def transfer(item, ref):
        i = INDEX[item]
        return pltpu.make_async_remote_copy(
            src_ref=ref, dst_ref=ref, send_sem=send_sem.at[i], recv_sem=recv_sem.at[i],
            device_id=hop[item[0]], device_id_type=MESH,
        )

    arrived = set()

    def need(line_, offset, half, c):
        item = ARRIVES.get((line_, far(offset), half, c))
        if item is not None and item not in arrived:
            arrived.add(item)
            transfer(item, block(*arrival(item), item)).wait_recv()

    shared = [
        pltpu.make_async_remote_copy(
            src_ref=t.at[0], dst_ref=tokens.at[i, pl.ds(half, count)],
            send_sem=tok_send.at[i], recv_sem=tok_recv.at[i], device_id=sibling, device_id_type=MESH,
        )
        for i, t in enumerate((grads_ref, acts_ref))
    ]
    theirs = pltpu.make_async_remote_copy(
        src_ref=member.at[core], dst_ref=member.at[core],
        send_sem=mem_send, recv_sem=mem_recv, device_id=sibling, device_id_type=MESH,
    )

    def multiply(line_, half, c, first):
        rows = (line if line_ == 0 else 1 - line) * RING
        left = gathered[c][pl.ds(rows, RING), half].reshape(RING * rank, UNIT * SIZES[c])
        into = pl.ds(pl.multiple_of(rows * rank, RING * rank), RING * rank)

        def tile(t, carry):
            some = pl.ds(pl.multiple_of(t * count, count), count)
            part = lax.dot_general(
                left, tokens[half, some, columns[c]], (((1,), (1,)), ((), ())),
                preferred_element_type=jnp.float32,
            )
            if first:
                proj[half, into, some] = part
            else:
                proj[half, into, some] += part
            return carry

        lax.fori_loop(0, CORES, tile, 0)

    other = pl.ds(pl.multiple_of((1 - core) * count, count), count)
    begun, counted = set(), set()
    for k, item in enumerate(ORDER):
        if k == SHARE:
            for copy in shared:
                copy.start()
            theirs.start()
        if item[0] != 2:
            for half in halves(item):
                need(item[1], item[2], half, item[3])
            transfer(item, block(item[1], item[2], item)).start()
            continue
        _, line_, half, c = item
        if half not in begun:
            begun.add(half)
            here[half].wait()
            pltpu.make_async_remote_copy(
                src_ref=(grads_ref, acts_ref)[half].at[0], dst_ref=tokens.at[half, other],
                send_sem=tok_send.at[half], recv_sem=tok_recv.at[half], device_id=sibling, device_id_type=MESH,
            ).wait_recv()
        for offset in range(RING):
            need(line_, offset if offset <= RING // 2 else offset - RING, half, c)
        multiply(line_, half, c, (line_, half) not in counted)
        counted.add((line_, half))

    pltpu.make_async_remote_copy(
        src_ref=member.at[1 - core], dst_ref=member.at[1 - core],
        send_sem=mem_send, recv_sem=mem_recv, device_id=sibling, device_id_type=MESH,
    ).wait_recv()
    queries = LINES * RING
    terms = (proj[0] * proj[1]).reshape(queries, rank, CORES * count).sum(axis=1)
    scores = sum(
        lax.dot_general(
            terms[:, t * count : (t + 1) * count], member[t], (((1,), (1,)), ((), ())),
            precision=lax.Precision.HIGHEST, preferred_element_type=jnp.float32,
        )
        for t in range(CORES)
    )
    each = queries // layers
    tile_row = lax.broadcasted_iota(jnp.int32, (8, scores.shape[1]), 0)
    tiles[...] = jnp.zeros_like(tiles)
    for to in range(layers):
        tile = jnp.zeros((8, scores.shape[1]), jnp.float32)
        for i in range(each):
            tile = jnp.where(tile_row == CORES * i + core, scores[to * each + i][None, :], tile)
        tiles[to, :, 0 : scores.shape[1]] = tile

    me = layer * CORES + core
    moves = []
    for step in range(1, layers * CORES):
        to = (me + step) % (layers * CORES)
        moves.append(
            pltpu.make_async_remote_copy(
                src_ref=tiles.at[to // CORES], dst_ref=landed.at[step],
                send_sem=tile_send.at[step], recv_sem=tile_recv.at[step],
                device_id=(device(line, ring, to % CORES), to // CORES), device_id_type=MESH,
            )
        )
    for move in moves:
        move.start()

    for item in SENDS:
        transfer(item, block(item[1], item[2], item)).wait_send()
    for copy in shared:
        copy.wait_send()
    theirs.wait_send()
    total = tiles[layer]
    for step in range(1, layers * CORES):
        moves[step - 1].wait_recv()
        total = total + landed[step]
    for move in moves:
        move.wait_send()
    wide = total[0 : CORES * each]
    result_ref[...] = jnp.where(core == 0, wide[:, 0:docs], wide[:, docs : 2 * docs])


def local(activations, backprops, out_factors, in_factors, doc_lengths):
    count, width = activations.shape[1:]
    rank = out_factors.shape[2]
    docs = doc_lengths.shape[1]
    layers = lax.axis_size("layer") * activations.shape[0]
    queries = LINES * RING
    scaling = 1.0 / math.sqrt(rank * layers * count / docs)
    hbm = pl.BlockSpec(memory_space=pl.ANY)
    dma = pltpu.SemaphoreType.DMA
    flops = 2 * 2 * queries * rank * CORES * count * width
    scores = pl.pallas_call(
        functools.partial(kernel, layers),
        out_shape=jax.ShapeDtypeStruct((CORES * queries // layers, docs), jnp.float32),
        in_specs=[pl.BlockSpec(memory_space=pltpu.SMEM), hbm, hbm, hbm, hbm],
        out_specs=pl.BlockSpec(memory_space=pltpu.VMEM),
        scratch_shapes=[
            pltpu.VMEM((2, CORES * count, width), jnp.bfloat16),
            pltpu.VMEM((2, queries * rank, CORES * count), jnp.float32),
            pltpu.VMEM((CORES, 8, count), jnp.float32),
            pltpu.VMEM((layers, 8, 128), jnp.float32),
            pltpu.VMEM((layers * CORES, 8, 128), jnp.float32),
            dma((len(SIZES), 2)),
            dma((2,)),
            dma((2,)),
            dma((2,)),
            dma((len(SENDS),)),
            dma((len(SENDS),)),
            dma,
            dma,
            dma((layers * CORES,)),
            dma((layers * CORES,)),
            *(pltpu.VMEM((queries, 2, rank, UNIT * size), jnp.bfloat16) for size in SIZES),
        ],
        compiler_params=pltpu.CompilerParams(
            collective_id=0, has_side_effects=True, vmem_limit_bytes=56 * 2**20
        ),
        cost_estimate=pl.CostEstimate(flops=flops, bytes_accessed=12 * 2**20, transcendentals=0),
        name="gather_scores",
    )(doc_lengths, activations, backprops, out_factors, in_factors)
    return scores * scaling


def solution(mesh):
    placed = (
        P("layer", "dp", None),
        P("layer", "dp", None),
        P("layer", "dp", None, None),
        P("layer", "dp", None, None),
        P("dp", None),
    )
    return jax.shard_map(
        local, mesh=mesh, in_specs=placed, out_specs=P("layer", "dp"), check_vma=False
    )
```

```python
import functools
import math

import jax
import jax.numpy as jnp
from jax import lax
from jax.experimental import pallas as pl
from jax.experimental.pallas import tpu as pltpu
from jax.sharding import PartitionSpec as P

MESH = pl.DeviceIdType.MESH
RING = 8
LINES = 2
CORES = 2
SHARE = 6
UNIT = 128
SIZES = (16, 14, 10)

ORDER = (
    (0, 0, 0, 1), (-1, 0, 0, 0), (1, 0, 0, 0), (0, 0, 0, 0), (1, 0, 0, 1), (0, 0, 0, 2),
    (-1, 0, 0, 1), (-1, 0, 1, 0), (1, 0, -1, 0), (0, 0, -1, 1), (1, 0, -1, 1), (1, 0, 0, 2),
    (-1, 0, 1, 1), (-1, 0, 0, 2), (0, 0, -2, 0), (-1, 0, 2, 0), (1, 0, -2, 1), (0, 0, 2, 1),
    (1, 0, -2, 0), (-1, 0, 2, 1), (1, 0, -1, 2), (-1, 0, 1, 2), (0, 0, -2, 1), (0, 0, 2, 0),
    (1, 0, -3, 1), (-1, 1, 2, 1), (-1, 1, 0, 0), (0, 0, 3, 0), (-1, 0, 2, 2), (0, 0, -3, 0),
    (1, 0, -2, 2), (1, 0, -3, 0), (1, 1, -2, 1), (2, 0, 0, 1), (-1, 0, 3, 0), (0, 0, 1, 1),
    (1, 1, 0, 0), (0, 0, -3, 2), (-1, 1, 3, 1), (0, 0, 3, 2), (-1, 1, 3, 0), (1, 0, -3, 2),
    (1, 1, -3, 1), (0, 0, -2, 2), (-1, 0, 3, 1), (2, 0, 0, 0), (1, 1, 0, 2), (0, 0, 2, 2),
    (-1, 0, 3, 2), (2, 0, 0, 2), (1, 1, -3, 0), (1, 1, -3, 2), (-1, 1, 0, 2), (2, 1, 1, 1),
    (2, 1, 1, 0), (-1, 1, 3, 2), (2, 0, 1, 0), (2, 1, 0, 1), (2, 0, 1, 1), (2, 0, 1, 2),
    (2, 1, 0, 0), (2, 1, 1, 2), (2, 1, 0, 2),
)
SENDS = tuple(item for item in ORDER if item[0] != 2)
INDEX = {item: i for i, item in enumerate(SENDS)}


def far(offset):
    return RING // 2 if abs(offset) == RING // 2 else offset


def halves(item):
    way, _, offset, _ = item
    if way and abs(offset - way) == RING // 2:
        return (0,) if way == 1 else (1,)
    return (0, 1)


def arrival(item):
    way, line, offset, _ = item
    return (1 - line, far(offset)) if way == 0 else (line, far(offset - way))


ARRIVES = {(*arrival(item), half, item[3]): item for item in SENDS for half in halves(item)}


def kernel(
    layers, lens_ref, acts_ref, grads_ref, outs_ref, ins_ref, result_ref,
    lens, tokens, proj, member, tiles, landed,
    lens_sem, own_sem, tok_sem, tok_send, tok_recv, send_sem, recv_sem, mem_send, mem_recv, tile_send, tile_recv,
    *gathered,
):
    dp, layer = lax.axis_index("dp"), lax.axis_index("layer")
    line, ring, core = dp // (RING * CORES), (dp // CORES) % RING, dp % CORES
    rank, width = outs_ref.shape[2], outs_ref.shape[3]
    count = acts_ref.shape[1]
    docs = lens_ref.shape[1]
    starts = [UNIT * sum(SIZES[:c]) for c in range(len(SIZES))]
    columns = [pl.ds(start, UNIT * size) for start, size in zip(starts, SIZES)]

    def device(line_, ring_, core_):
        return (line_ * RING + ring_) * CORES + core_

    up = (device(line, (ring + 1) % RING, core), layer)
    down = (device(line, (ring + RING - 1) % RING, core), layer)
    across = (device(1 - line, ring, core), layer)
    sibling = (device(line, ring, 1 - core), layer)
    hop = {1: up, -1: down, 0: across}

    barrier = pltpu.get_barrier_semaphore()
    for target in (up, down, across):
        pl.semaphore_signal(barrier, inc=1, device_id=target, device_id_type=MESH)

    mine = line * RING + ring
    half = pl.multiple_of(core * count, count)
    own = [
        pltpu.make_async_copy(f.at[0, 0, :, columns[c]], gathered[c].at[mine, i], own_sem.at[c, i])
        for c in range(len(SIZES))
        for i, f in enumerate((outs_ref, ins_ref))
    ]
    here = [
        pltpu.make_async_copy(t.at[0], tokens.at[i, pl.ds(half, count)], tok_sem.at[i])
        for i, t in enumerate((grads_ref, acts_ref))
    ]
    for copy in own[:2]:
        copy.start()
    for step in range(1, layers * CORES):
        to = (layer * CORES + core + step) % (layers * CORES)
        pl.semaphore_signal(
            barrier, inc=1, device_id=(device(line, ring, to % CORES), to // CORES), device_id_type=MESH
        )

    lengths = pltpu.make_async_copy(lens_ref, lens, lens_sem)
    lengths.start()
    for copy in own[2:]:
        copy.start()
    tiles[...] = jnp.zeros_like(tiles)
    for copy in own[:2]:
        copy.wait()
    pl.semaphore_wait(barrier, 3 + layers * CORES - 1)

    def block(line_, offset, item):
        part = halves(item)
        slot = (line if line_ == 0 else 1 - line) * RING + (ring + offset + RING) % RING
        return gathered[item[3]].at[slot, pl.ds(part[0], len(part))]

    def transfer(item, ref):
        i = INDEX[item]
        return pltpu.make_async_remote_copy(
            src_ref=ref, dst_ref=ref, send_sem=send_sem.at[i], recv_sem=recv_sem.at[i],
            device_id=hop[item[0]], device_id_type=MESH,
        )

    arrived = set()

    def need(line_, offset, half, c):
        item = ARRIVES.get((line_, far(offset), half, c))
        if item is not None and item not in arrived:
            arrived.add(item)
            transfer(item, block(*arrival(item), item)).wait_recv()

    shared = [
        pltpu.make_async_remote_copy(
            src_ref=t.at[0], dst_ref=tokens.at[i, pl.ds(half, count)],
            send_sem=tok_send.at[i], recv_sem=tok_recv.at[i], device_id=sibling, device_id_type=MESH,
        )
        for i, t in enumerate((grads_ref, acts_ref))
    ]
    theirs = pltpu.make_async_remote_copy(
        src_ref=member.at[core], dst_ref=member.at[core],
        send_sem=mem_send, recv_sem=mem_recv, device_id=sibling, device_id_type=MESH,
    )

    def multiply(line_, half, c, first):
        rows = (line if line_ == 0 else 1 - line) * RING
        left = gathered[c][pl.ds(rows, RING), half].reshape(RING * rank, UNIT * SIZES[c])
        into = pl.ds(pl.multiple_of(rows * rank, RING * rank), RING * rank)

        def tile(t, carry):
            some = pl.ds(pl.multiple_of(t * count, count), count)
            part = lax.dot_general(
                left, tokens[half, some, columns[c]], (((1,), (1,)), ((), ())),
                preferred_element_type=jnp.float32,
            )
            if first:
                proj[half, into, some] = part
            else:
                proj[half, into, some] += part
            return carry

        lax.fori_loop(0, CORES, tile, 0)

    me, everyone = layer * CORES + core, layers * CORES
    each = LINES * RING // layers
    targets = RING // each

    def give(to, sender):
        return pltpu.make_async_remote_copy(
            src_ref=tiles.at[to // CORES], dst_ref=landed.at[sender],
            send_sem=tile_send.at[to], recv_sem=tile_recv.at[sender],
            device_id=(device(line, ring, to % CORES), to // CORES), device_id_type=MESH,
        )

    def finish(line_, first):
        if first:
            pltpu.make_async_remote_copy(
                src_ref=member.at[1 - core], dst_ref=member.at[1 - core],
                send_sem=mem_send, recv_sem=mem_recv, device_id=sibling, device_id_type=MESH,
            ).wait_recv()
        which = line if line_ == 0 else 1 - line
        rows = pl.ds(pl.multiple_of(which * RING * rank, RING * rank), RING * rank)
        terms = (proj[0, rows] * proj[1, rows]).reshape(RING, rank, CORES * count).sum(axis=1)
        scores = sum(
            lax.dot_general(
                terms[:, t * count : (t + 1) * count], member[t], (((1,), (1,)), ((), ())),
                precision=lax.Precision.HIGHEST, preferred_element_type=jnp.float32,
            )
            for t in range(CORES)
        )
        wide = scores.shape[1]
        by_target = scores.reshape(targets, each, wide)
        for i in range(each):
            for p in range(CORES):
                tiles[pl.ds(which * targets, targets), CORES * i + p, 0:wide] = jnp.where(core == p, by_target[:, i], 0.0)
        for k in range(targets * CORES):
            to = which * targets * CORES + k

            @pl.when(to != me)
            def _():
                give(to, me).start()

    def members():
        lengths.wait()
        position = lax.broadcasted_iota(jnp.int32, (8, count), 1)
        row = lax.broadcasted_iota(jnp.int32, (8, count), 0)
        held = jnp.zeros((8, count), jnp.float32)
        first = jnp.int32(0)
        for d in range(docs):
            after = first + lens[0, d]
            inside = (row == core * docs + d) & (position >= first) & (position < after)
            held = jnp.where(inside, 1.0, held)
            first = after
        member[core] = held

    other = pl.ds(pl.multiple_of((1 - core) * count, count), count)
    finished = []
    begun, counted, loaded = set(), {}, {0}
    for k, item in enumerate(ORDER):
        if k == SHARE:
            for copy in here + shared:
                copy.start()
            members()
            theirs.start()
        if item[0] != 2:
            if item[3] not in loaded and item[1:3] == (0, 0):
                loaded.add(item[3])
                for copy in own[2 * item[3] : 2 * item[3] + 2]:
                    copy.wait()
            for half in halves(item):
                need(item[1], item[2], half, item[3])
            transfer(item, block(item[1], item[2], item)).start()
            continue
        _, line_, half, c = item
        if half not in begun:
            begun.add(half)
            here[half].wait()
            pltpu.make_async_remote_copy(
                src_ref=(grads_ref, acts_ref)[half].at[0], dst_ref=tokens.at[half, other],
                send_sem=tok_send.at[half], recv_sem=tok_recv.at[half], device_id=sibling, device_id_type=MESH,
            ).wait_recv()
        for offset in range(RING):
            need(line_, offset if offset <= RING // 2 else offset - RING, half, c)
        multiply(line_, half, c, (line_, half) not in counted.values())
        counted[item] = (line_, half)
        if sum(way[0] == line_ for way in counted.values()) == 2 * len(SIZES):
            finish(line_, len(finished) == 0)
            finished.append(line_)

    for item in SENDS:
        transfer(item, block(item[1], item[2], item)).wait_send()
    for copy in shared:
        copy.wait_send()
    theirs.wait_send()
    total = tiles[layer]
    for step in range(1, everyone):
        give((me + step) % everyone, (me + step) % everyone).wait_recv()
        total = total + landed[(me + step) % everyone]
    for step in range(1, everyone):
        give((me + step) % everyone, me).wait_send()
    rows = total[0 : CORES * each]
    result_ref[...] = jnp.where(core == 0, rows[:, 0:docs], rows[:, docs : 2 * docs])


def local(activations, backprops, out_factors, in_factors, doc_lengths):
    count, width = activations.shape[1:]
    rank = out_factors.shape[2]
    docs = doc_lengths.shape[1]
    layers = lax.axis_size("layer") * activations.shape[0]
    queries = LINES * RING
    scaling = 1.0 / math.sqrt(rank * layers * count / docs)
    hbm = pl.BlockSpec(memory_space=pl.ANY)
    dma = pltpu.SemaphoreType.DMA
    flops = 2 * 2 * queries * rank * CORES * count * width
    scores = pl.pallas_call(
        functools.partial(kernel, layers),
        out_shape=jax.ShapeDtypeStruct((CORES * queries // layers, docs), jnp.float32),
        in_specs=[hbm] * 5,
        out_specs=pl.BlockSpec(memory_space=pltpu.VMEM),
        scratch_shapes=[
            pltpu.SMEM((1, docs), jnp.int32),
            pltpu.VMEM((2, CORES * count, width), jnp.bfloat16),
            pltpu.VMEM((2, queries * rank, CORES * count), jnp.float32),
            pltpu.VMEM((CORES, 8, count), jnp.float32),
            pltpu.VMEM((layers, 8, 128), jnp.float32),
            pltpu.VMEM((layers * CORES, 8, 128), jnp.float32),
            dma,
            dma((len(SIZES), 2)),
            dma((2,)),
            dma((2,)),
            dma((2,)),
            dma((len(SENDS),)),
            dma((len(SENDS),)),
            dma,
            dma,
            dma((layers * CORES,)),
            dma((layers * CORES,)),
            *(pltpu.VMEM((queries, 2, rank, UNIT * size), jnp.bfloat16) for size in SIZES),
        ],
        compiler_params=pltpu.CompilerParams(
            collective_id=0, has_side_effects=True, vmem_limit_bytes=56 * 2**20
        ),
        cost_estimate=pl.CostEstimate(flops=flops, bytes_accessed=12 * 2**20, transcendentals=0),
        name="gather_scores",
    )(doc_lengths, activations, backprops, out_factors, in_factors)
    return scores * scaling


def solution(mesh):
    placed = (
        P("layer", "dp", None),
        P("layer", "dp", None),
        P("layer", "dp", None, None),
        P("layer", "dp", None, None),
        P("dp", None),
    )
    return jax.shard_map(
        local, mesh=mesh, in_specs=placed, out_specs=P("layer", "dp"), check_vma=False
    )
```

```python
import functools
import math

import jax
import jax.numpy as jnp
from jax import lax
from jax.experimental import pallas as pl
from jax.experimental.pallas import tpu as pltpu
from jax.sharding import PartitionSpec as P

MESH = pl.DeviceIdType.MESH
RING = 8
LINES = 2
CORES = 2
SHARE = 6
UNIT = 128
SIZES = (18, 14, 8)

ORDER = (
    (0, 0, 0, 2), (0, 0, 0, 0), (1, 0, 0, 1), (-1, 0, 0, 1), (1, 0, 0, 2), (1, 0, 0, 0),
    (-1, 0, 0, 0), (-1, 0, 1, 1), (0, 0, -1, 1), (0, 0, 1, 1), (1, 0, -1, 2), (-1, 0, 1, 0),
    (0, 0, 0, 1), (1, 0, -1, 0), (1, 0, -1, 1), (-1, 0, 0, 2), (0, 0, 2, 1), (-1, 0, 2, 1),
    (0, 0, 2, 0), (1, 0, -2, 0), (-1, 0, 1, 2), (1, 0, -2, 1), (-1, 1, 2, 1), (1, 0, -2, 2),
    (0, 0, -2, 1), (0, 0, -2, 0), (0, 0, -3, 0), (-1, 0, 2, 2), (-1, 0, 2, 0), (1, 1, 0, 0),
    (1, 0, -3, 2), (1, 0, -3, 1), (-1, 0, 3, 1), (-1, 0, 3, 2), (-1, 1, 3, 1), (-1, 0, 3, 0),
    (0, 0, 3, 0), (1, 1, -2, 1), (2, 0, 0, 1), (1, 0, -3, 0), (0, 0, 3, 2), (1, 1, -3, 0),
    (0, 0, -3, 2), (-1, 1, 0, 0), (2, 0, 1, 0), (0, 0, 2, 2), (1, 1, 0, 2), (2, 0, 0, 2),
    (-1, 1, 3, 0), (2, 0, 1, 1), (0, 0, -2, 2), (2, 1, 1, 1), (2, 0, 1, 2), (-1, 1, 0, 2),
    (-1, 1, 3, 2), (1, 1, -3, 1), (2, 1, 0, 0), (1, 1, -3, 2), (2, 0, 0, 0), (2, 1, 1, 0),
    (2, 1, 0, 1), (2, 1, 0, 2), (2, 1, 1, 2),
)
SENDS = tuple(item for item in ORDER if item[0] != 2)
INDEX = {item: i for i, item in enumerate(SENDS)}


def far(offset):
    return RING // 2 if abs(offset) == RING // 2 else offset


def halves(item):
    way, _, offset, _ = item
    if way and abs(offset - way) == RING // 2:
        return (0,) if way == 1 else (1,)
    return (0, 1)


def arrival(item):
    way, line, offset, _ = item
    return (1 - line, far(offset)) if way == 0 else (line, far(offset - way))


ARRIVES = {(*arrival(item), half, item[3]): item for item in SENDS for half in halves(item)}


def kernel(
    layers, lens_ref, acts_ref, grads_ref, outs_ref, ins_ref, result_ref,
    lens, tokens, proj, member, tiles, landed,
    lens_sem, own_sem, tok_sem, tok_send, tok_recv, send_sem, recv_sem, mem_send, mem_recv, tile_send, tile_recv,
    *gathered,
):
    dp, layer = lax.axis_index("dp"), lax.axis_index("layer")
    line, ring, core = dp // (RING * CORES), (dp // CORES) % RING, dp % CORES
    rank, width = outs_ref.shape[2], outs_ref.shape[3]
    count = acts_ref.shape[1]
    docs = lens_ref.shape[1]
    starts = [UNIT * sum(SIZES[:c]) for c in range(len(SIZES))]
    columns = [pl.ds(start, UNIT * size) for start, size in zip(starts, SIZES)]

    def device(line_, ring_, core_):
        return (line_ * RING + ring_) * CORES + core_

    up = (device(line, (ring + 1) % RING, core), layer)
    down = (device(line, (ring + RING - 1) % RING, core), layer)
    across = (device(1 - line, ring, core), layer)
    sibling = (device(line, ring, 1 - core), layer)
    hop = {1: up, -1: down, 0: across}

    barrier = pltpu.get_barrier_semaphore()
    for target in (up, down, across):
        pl.semaphore_signal(barrier, inc=1, device_id=target, device_id_type=MESH)

    mine = line * RING + ring
    half = pl.multiple_of(core * count, count)
    own = [
        pltpu.make_async_copy(f.at[0, 0, :, columns[c]], gathered[c].at[mine, i], own_sem.at[c, i])
        for c in range(len(SIZES))
        for i, f in enumerate((outs_ref, ins_ref))
    ]
    here = [
        pltpu.make_async_copy(t.at[0], tokens.at[i, pl.ds(half, count)], tok_sem.at[i])
        for i, t in enumerate((grads_ref, acts_ref))
    ]
    for copy in own[:2]:
        copy.start()
    for step in range(1, layers * CORES):
        to = (layer * CORES + core + step) % (layers * CORES)
        pl.semaphore_signal(
            barrier, inc=1, device_id=(device(line, ring, to % CORES), to // CORES), device_id_type=MESH
        )

    lengths = pltpu.make_async_copy(lens_ref, lens, lens_sem)
    lengths.start()
    for copy in own[2:]:
        copy.start()
    tiles[...] = jnp.zeros_like(tiles)
    for copy in own[:2]:
        copy.wait()
    pl.semaphore_wait(barrier, 3 + layers * CORES - 1)

    def block(line_, offset, item):
        part = halves(item)
        slot = (line if line_ == 0 else 1 - line) * RING + (ring + offset + RING) % RING
        return gathered[item[3]].at[slot, pl.ds(part[0], len(part))]

    def transfer(item, ref):
        i = INDEX[item]
        return pltpu.make_async_remote_copy(
            src_ref=ref, dst_ref=ref, send_sem=send_sem.at[i], recv_sem=recv_sem.at[i],
            device_id=hop[item[0]], device_id_type=MESH,
        )

    arrived = set()

    def need(line_, offset, half, c):
        item = ARRIVES.get((line_, far(offset), half, c))
        if item is not None and item not in arrived:
            arrived.add(item)
            transfer(item, block(*arrival(item), item)).wait_recv()

    shared = [
        pltpu.make_async_remote_copy(
            src_ref=t.at[0], dst_ref=tokens.at[i, pl.ds(half, count)],
            send_sem=tok_send.at[i], recv_sem=tok_recv.at[i], device_id=sibling, device_id_type=MESH,
        )
        for i, t in enumerate((grads_ref, acts_ref))
    ]
    theirs = pltpu.make_async_remote_copy(
        src_ref=member.at[core], dst_ref=member.at[core],
        send_sem=mem_send, recv_sem=mem_recv, device_id=sibling, device_id_type=MESH,
    )

    def multiply(line_, half, c, first):
        rows = (line if line_ == 0 else 1 - line) * RING
        left = gathered[c][pl.ds(rows, RING), half].reshape(RING * rank, UNIT * SIZES[c])
        into = pl.ds(pl.multiple_of(rows * rank, RING * rank), RING * rank)

        def tile(t, carry):
            some = pl.ds(pl.multiple_of(t * count, count), count)
            part = lax.dot_general(
                left, tokens[half, some, columns[c]], (((1,), (1,)), ((), ())),
                preferred_element_type=jnp.float32,
            )
            if first:
                proj[half, into, some] = part
            else:
                proj[half, into, some] += part
            return carry

        lax.fori_loop(0, CORES, tile, 0, unroll=c == len(SIZES) - 1)

    me, everyone = layer * CORES + core, layers * CORES
    each = LINES * RING // layers
    targets = RING // each

    def give(to, sender):
        return pltpu.make_async_remote_copy(
            src_ref=tiles.at[to // CORES], dst_ref=landed.at[sender],
            send_sem=tile_send.at[to], recv_sem=tile_recv.at[sender],
            device_id=(device(line, ring, to % CORES), to // CORES), device_id_type=MESH,
        )

    def finish(line_, first):
        if first:
            pltpu.make_async_remote_copy(
                src_ref=member.at[1 - core], dst_ref=member.at[1 - core],
                send_sem=mem_send, recv_sem=mem_recv, device_id=sibling, device_id_type=MESH,
            ).wait_recv()
        which = line if line_ == 0 else 1 - line
        rows = pl.ds(pl.multiple_of(which * RING * rank, RING * rank), RING * rank)
        terms = (proj[0, rows] * proj[1, rows]).reshape(RING, rank, CORES * count).sum(axis=1)
        lane = lax.broadcasted_iota(jnp.int32, (RING, tiles.shape[2]), 1)
        scores = jnp.zeros(lane.shape, jnp.float32)
        for d in range(CORES * docs):
            t = d // docs
            mine_of = terms[:, t * count : (t + 1) * count] * member[t, d : d + 1]
            scores = jnp.where(lane == d, mine_of.sum(axis=1, keepdims=True), scores)
        by_target = scores.reshape(targets, each, lane.shape[1])
        for i in range(each):
            for p in range(CORES):
                tiles[pl.ds(which * targets, targets), CORES * i + p, :] = jnp.where(core == p, by_target[:, i], 0.0)
        for k in range(targets * CORES):
            to = which * targets * CORES + k

            @pl.when(to != me)
            def _():
                give(to, me).start()

    def members():
        lengths.wait()
        position = lax.broadcasted_iota(jnp.int32, (8, count), 1)
        row = lax.broadcasted_iota(jnp.int32, (8, count), 0)
        held = jnp.zeros((8, count), jnp.float32)
        first = jnp.int32(0)
        for d in range(docs):
            after = first + lens[0, d]
            inside = (row == core * docs + d) & (position >= first) & (position < after)
            held = jnp.where(inside, 1.0, held)
            first = after
        member[core] = held

    other = pl.ds(pl.multiple_of((1 - core) * count, count), count)
    finished = []
    begun, counted, loaded = set(), {}, {0}
    for k, item in enumerate(ORDER):
        if k == SHARE:
            for copy in here + shared:
                copy.start()
            members()
            theirs.start()
        if item[0] != 2:
            if item[3] not in loaded and item[1:3] == (0, 0):
                loaded.add(item[3])
                for copy in own[2 * item[3] : 2 * item[3] + 2]:
                    copy.wait()
            for half in halves(item):
                need(item[1], item[2], half, item[3])
            transfer(item, block(item[1], item[2], item)).start()
            continue
        _, line_, half, c = item
        if half not in begun:
            begun.add(half)
            here[half].wait()
            pltpu.make_async_remote_copy(
                src_ref=(grads_ref, acts_ref)[half].at[0], dst_ref=tokens.at[half, other],
                send_sem=tok_send.at[half], recv_sem=tok_recv.at[half], device_id=sibling, device_id_type=MESH,
            ).wait_recv()
        for offset in range(RING):
            need(line_, offset if offset <= RING // 2 else offset - RING, half, c)
        multiply(line_, half, c, (line_, half) not in counted.values())
        counted[item] = (line_, half)
        if sum(way[0] == line_ for way in counted.values()) == 2 * len(SIZES):
            finish(line_, len(finished) == 0)
            finished.append(line_)

    for item in SENDS:
        transfer(item, block(item[1], item[2], item)).wait_send()
    for copy in shared:
        copy.wait_send()
    theirs.wait_send()
    total = tiles[layer]
    for step in range(1, everyone):
        give((me + step) % everyone, (me + step) % everyone).wait_recv()
        total = total + landed[(me + step) % everyone]
    for step in range(1, everyone):
        give((me + step) % everyone, me).wait_send()
    rows = total[0 : CORES * each]
    result_ref[...] = jnp.where(core == 0, rows[:, 0:docs], rows[:, docs : 2 * docs])


def local(activations, backprops, out_factors, in_factors, doc_lengths):
    count, width = activations.shape[1:]
    rank = out_factors.shape[2]
    docs = doc_lengths.shape[1]
    layers = lax.axis_size("layer") * activations.shape[0]
    queries = LINES * RING
    scaling = 1.0 / math.sqrt(rank * layers * count / docs)
    hbm = pl.BlockSpec(memory_space=pl.ANY)
    dma = pltpu.SemaphoreType.DMA
    flops = 2 * 2 * queries * rank * CORES * count * width
    scores = pl.pallas_call(
        functools.partial(kernel, layers),
        out_shape=jax.ShapeDtypeStruct((CORES * queries // layers, docs), jnp.float32),
        in_specs=[hbm] * 5,
        out_specs=pl.BlockSpec(memory_space=pltpu.VMEM),
        scratch_shapes=[
            pltpu.SMEM((1, docs), jnp.int32),
            pltpu.VMEM((2, CORES * count, width), jnp.bfloat16),
            pltpu.VMEM((2, queries * rank, CORES * count), jnp.float32),
            pltpu.VMEM((CORES, 8, count), jnp.float32),
            pltpu.VMEM((layers, 8, 128), jnp.float32),
            pltpu.VMEM((layers * CORES, 8, 128), jnp.float32),
            dma,
            dma((len(SIZES), 2)),
            dma((2,)),
            dma((2,)),
            dma((2,)),
            dma((len(SENDS),)),
            dma((len(SENDS),)),
            dma,
            dma,
            dma((layers * CORES,)),
            dma((layers * CORES,)),
            *(pltpu.VMEM((queries, 2, rank, UNIT * size), jnp.bfloat16) for size in SIZES),
        ],
        compiler_params=pltpu.CompilerParams(
            collective_id=0, has_side_effects=True, vmem_limit_bytes=56 * 2**20
        ),
        cost_estimate=pl.CostEstimate(flops=flops, bytes_accessed=12 * 2**20, transcendentals=0),
        name="gather_scores",
    )(doc_lengths, activations, backprops, out_factors, in_factors)
    return scores * scaling


def solution(mesh):
    placed = (
        P("layer", "dp", None),
        P("layer", "dp", None),
        P("layer", "dp", None, None),
        P("layer", "dp", None, None),
        P("dp", None),
    )
    return jax.shard_map(
        local, mesh=mesh, in_specs=placed, out_specs=P("layer", "dp"), check_vma=False
    )
```

```python
import functools
import math

import jax
import jax.numpy as jnp
from jax import lax
from jax.experimental import pallas as pl
from jax.experimental.pallas import tpu as pltpu
from jax.sharding import PartitionSpec as P

MESH = pl.DeviceIdType.MESH
RING = 8
LINES = 2
CORES = 2
SHARE = 6
UNIT = 128
SIZES = (18, 14, 8)

ORDER = (
    (0, 0, 0, 2), (0, 0, 0, 0), (1, 0, 0, 1), (-1, 0, 0, 1), (1, 0, 0, 2), (1, 0, 0, 0),
    (-1, 0, 0, 0), (-1, 0, 1, 1), (0, 0, -1, 1), (0, 0, 1, 1), (1, 0, -1, 2), (-1, 0, 1, 0),
    (0, 0, 0, 1), (1, 0, -1, 0), (1, 0, -1, 1), (-1, 0, 0, 2), (0, 0, 2, 1), (-1, 0, 2, 1),
    (0, 0, 2, 0), (1, 0, -2, 0), (-1, 0, 1, 2), (1, 0, -2, 1), (-1, 1, 2, 1), (1, 0, -2, 2),
    (0, 0, -2, 1), (0, 0, -2, 0), (0, 0, -3, 0), (-1, 0, 2, 2), (-1, 0, 2, 0), (1, 1, 0, 0),
    (1, 0, -3, 2), (1, 0, -3, 1), (-1, 0, 3, 1), (-1, 0, 3, 2), (-1, 1, 3, 1), (-1, 0, 3, 0),
    (0, 0, 3, 0), (1, 1, -2, 1), (2, 0, 0, 1), (1, 0, -3, 0), (0, 0, 3, 2), (1, 1, -3, 0),
    (0, 0, -3, 2), (-1, 1, 0, 0), (2, 0, 1, 0), (0, 0, 2, 2), (1, 1, 0, 2), (2, 0, 0, 2),
    (-1, 1, 3, 0), (2, 0, 1, 1), (0, 0, -2, 2), (2, 1, 1, 1), (2, 0, 1, 2), (-1, 1, 0, 2),
    (-1, 1, 3, 2), (1, 1, -3, 1), (2, 1, 0, 0), (1, 1, -3, 2), (2, 0, 0, 0), (2, 1, 1, 0),
    (2, 1, 0, 1), (2, 1, 0, 2), (2, 1, 1, 2),
)
SENDS = tuple(item for item in ORDER if item[0] != 2)
INDEX = {item: i for i, item in enumerate(SENDS)}


def far(offset):
    return RING // 2 if abs(offset) == RING // 2 else offset


def halves(item):
    way, _, offset, _ = item
    if way and abs(offset - way) == RING // 2:
        return (0,) if way == 1 else (1,)
    return (0, 1)


def arrival(item):
    way, line, offset, _ = item
    return (1 - line, far(offset)) if way == 0 else (line, far(offset - way))


ARRIVES = {(*arrival(item), half, item[3]): item for item in SENDS for half in halves(item)}


def kernel(
    layers, lens_ref, acts_ref, grads_ref, outs_ref, ins_ref, result_ref,
    lens, shown, tokens, proj, member, tiles, landed,
    lens_sem, own_sem, tok_sem, tok_send, tok_recv, send_sem, recv_sem, mem_send, mem_recv, tile_send, tile_recv,
    *gathered,
):
    dp, layer = lax.axis_index("dp"), lax.axis_index("layer")
    line, ring, core = dp // (RING * CORES), (dp // CORES) % RING, dp % CORES
    rank, width = outs_ref.shape[2], outs_ref.shape[3]
    count = acts_ref.shape[1]
    docs = lens_ref.shape[1]
    starts = [UNIT * sum(SIZES[:c]) for c in range(len(SIZES))]
    columns = [pl.ds(start, UNIT * size) for start, size in zip(starts, SIZES)]

    def device(line_, ring_, core_):
        return (line_ * RING + ring_) * CORES + core_

    up = (device(line, (ring + 1) % RING, core), layer)
    down = (device(line, (ring + RING - 1) % RING, core), layer)
    across = (device(1 - line, ring, core), layer)
    sibling = (device(line, ring, 1 - core), layer)
    hop = {1: up, -1: down, 0: across}

    barrier = pltpu.get_barrier_semaphore()
    for target in (up, down, across):
        pl.semaphore_signal(barrier, inc=1, device_id=target, device_id_type=MESH)

    mine = line * RING + ring
    half = pl.multiple_of(core * count, count)
    own = [
        pltpu.make_async_copy(f.at[0, 0, :, columns[c]], gathered[c].at[mine, i], own_sem.at[c, i])
        for c in range(len(SIZES))
        for i, f in enumerate((outs_ref, ins_ref))
    ]
    here = [
        pltpu.make_async_copy(t.at[0], tokens.at[i, pl.ds(half, count)], tok_sem.at[i])
        for i, t in enumerate((grads_ref, acts_ref))
    ]
    for copy in own[:2]:
        copy.start()
    for step in range(1, layers * CORES):
        to = (layer * CORES + core + step) % (layers * CORES)
        pl.semaphore_signal(
            barrier, inc=1, device_id=(device(line, ring, to % CORES), to // CORES), device_id_type=MESH
        )

    lengths = pltpu.make_async_copy(lens_ref, lens, lens_sem)
    lengths.start()
    for copy in own[2:]:
        copy.start()
    tiles[...] = jnp.zeros_like(tiles)
    for copy in own[:2]:
        copy.wait()
    pl.semaphore_wait(barrier, 3 + layers * CORES - 1)

    def block(line_, offset, item):
        part = halves(item)
        slot = (line if line_ == 0 else 1 - line) * RING + (ring + offset + RING) % RING
        return gathered[item[3]].at[slot, pl.ds(part[0], len(part))]

    def transfer(item, ref):
        i = INDEX[item]
        return pltpu.make_async_remote_copy(
            src_ref=ref, dst_ref=ref, send_sem=send_sem.at[i], recv_sem=recv_sem.at[i],
            device_id=hop[item[0]], device_id_type=MESH,
        )

    arrived = set()

    def need(line_, offset, half, c):
        item = ARRIVES.get((line_, far(offset), half, c))
        if item is not None and item not in arrived:
            arrived.add(item)
            transfer(item, block(*arrival(item), item)).wait_recv()

    shared = [
        pltpu.make_async_remote_copy(
            src_ref=t.at[0], dst_ref=tokens.at[i, pl.ds(half, count)],
            send_sem=tok_send.at[i], recv_sem=tok_recv.at[i], device_id=sibling, device_id_type=MESH,
        )
        for i, t in enumerate((grads_ref, acts_ref))
    ]
    theirs = pltpu.make_async_remote_copy(
        src_ref=member.at[core], dst_ref=member.at[core],
        send_sem=mem_send, recv_sem=mem_recv, device_id=sibling, device_id_type=MESH,
    )

    def multiply(line_, half, c, first):
        rows = (line if line_ == 0 else 1 - line) * RING
        left = gathered[c][pl.ds(rows, RING), half].reshape(RING * rank, UNIT * SIZES[c])
        into = pl.ds(pl.multiple_of(rows * rank, RING * rank), RING * rank)

        def tile(t, carry):
            some = pl.ds(pl.multiple_of(t * count, count), count)
            part = lax.dot_general(
                left, tokens[half, some, columns[c]], (((1,), (1,)), ((), ())),
                preferred_element_type=jnp.float32,
            )
            if first:
                proj[half, into, some] = part
            else:
                proj[half, into, some] += part
            return carry

        lax.fori_loop(0, CORES, tile, 0, unroll=c == len(SIZES) - 1)

    me, everyone = layer * CORES + core, layers * CORES
    each = LINES * RING // layers
    targets = RING // each

    def give(to, sender):
        return pltpu.make_async_remote_copy(
            src_ref=tiles.at[to // CORES], dst_ref=landed.at[sender],
            send_sem=tile_send.at[to], recv_sem=tile_recv.at[sender],
            device_id=(device(line, ring, to % CORES), to // CORES), device_id_type=MESH,
        )

    def finish(line_, first):
        if first:
            pltpu.make_async_remote_copy(
                src_ref=member.at[1 - core], dst_ref=member.at[1 - core],
                send_sem=mem_send, recv_sem=mem_recv, device_id=sibling, device_id_type=MESH,
            ).wait_recv()
        which = line if line_ == 0 else 1 - line
        rows = pl.ds(pl.multiple_of(which * RING * rank, RING * rank), RING * rank)
        terms = (proj[0, rows] * proj[1, rows]).reshape(RING, rank, CORES * count).sum(axis=1)
        lane = lax.broadcasted_iota(jnp.int32, (RING, tiles.shape[2]), 1)
        scores = jnp.zeros(lane.shape, jnp.float32)
        for d in range(CORES * docs):
            t = d // docs
            mine_of = terms[:, t * count : (t + 1) * count] * member[t, d : d + 1]
            scores = jnp.where(lane == d, mine_of.sum(axis=1, keepdims=True), scores)
        by_target = scores.reshape(targets, each, lane.shape[1])
        for i in range(each):
            for p in range(CORES):
                tiles[pl.ds(which * targets, targets), CORES * i + p, :] = jnp.where(core == p, by_target[:, i], 0.0)
        for k in range(targets * CORES):
            to = which * targets * CORES + k

            @pl.when(to != me)
            def _():
                give(to, me).start()

    def members():
        lengths.wait()
        position = lax.broadcasted_iota(jnp.int32, (8, count), 1)
        row = lax.broadcasted_iota(jnp.int32, (8, count), 0)
        held = jnp.zeros((8, count), jnp.float32)
        first = jnp.int32(0)
        for d in range(docs):
            after = first + lens[0, d]
            inside = (row == core * docs + d) & (position >= first) & (position < after)
            held = jnp.where(inside, 1.0, held)
            first = after
        member[core] = held

    other = pl.ds(pl.multiple_of((1 - core) * count, count), count)
    finished = []
    begun, counted, loaded = set(), {}, {0}
    for k, item in enumerate(ORDER):
        if k == SHARE:
            for copy in here + shared:
                copy.start()
            members()
            theirs.start()
        if item[0] != 2:
            if item[3] not in loaded and item[1:3] == (0, 0):
                loaded.add(item[3])
                for copy in own[2 * item[3] : 2 * item[3] + 2]:
                    copy.wait()
            for half in halves(item):
                need(item[1], item[2], half, item[3])
            transfer(item, block(item[1], item[2], item)).start()
            continue
        _, line_, half, c = item
        if half not in begun:
            begun.add(half)
            here[half].wait()
            pltpu.make_async_remote_copy(
                src_ref=(grads_ref, acts_ref)[half].at[0], dst_ref=tokens.at[half, other],
                send_sem=tok_send.at[half], recv_sem=tok_recv.at[half], device_id=sibling, device_id_type=MESH,
            ).wait_recv()
        for offset in range(RING):
            need(line_, offset if offset <= RING // 2 else offset - RING, half, c)
        multiply(line_, half, c, (line_, half) not in counted.values())
        counted[item] = (line_, half)
        if sum(way[0] == line_ for way in counted.values()) == 2 * len(SIZES):
            finish(line_, len(finished) == 0)
            finished.append(line_)

    for item in SENDS:
        transfer(item, block(item[1], item[2], item)).wait_send()
    for copy in shared:
        copy.wait_send()
    theirs.wait_send()
    total = tiles[layer]
    for step in range(1, everyone):
        give((me + step) % everyone, (me + step) % everyone).wait_recv()
        total = total + landed[(me + step) % everyone]
    for step in range(1, everyone):
        give((me + step) % everyone, me).wait_send()
    rows = total[0 : CORES * each]
    shown[...] = jnp.where(core == 0, rows[:, 0:docs], rows[:, docs : 2 * docs])
    answer = pltpu.make_async_copy(shown, result_ref, lens_sem)
    answer.start()
    answer.wait()


def local(activations, backprops, out_factors, in_factors, doc_lengths):
    count, width = activations.shape[1:]
    rank = out_factors.shape[2]
    docs = doc_lengths.shape[1]
    layers = lax.axis_size("layer") * activations.shape[0]
    queries = LINES * RING
    scaling = 1.0 / math.sqrt(rank * layers * count / docs)
    hbm = pl.BlockSpec(memory_space=pl.ANY)
    dma = pltpu.SemaphoreType.DMA
    flops = 2 * 2 * queries * rank * CORES * count * width
    scores = pl.pallas_call(
        functools.partial(kernel, layers),
        out_shape=jax.ShapeDtypeStruct((CORES * queries // layers, docs), jnp.float32),
        in_specs=[hbm] * 5,
        out_specs=hbm,
        scratch_shapes=[
            pltpu.SMEM((1, docs), jnp.int32),
            pltpu.VMEM((CORES * queries // layers, docs), jnp.float32),
            pltpu.VMEM((2, CORES * count, width), jnp.bfloat16),
            pltpu.VMEM((2, queries * rank, CORES * count), jnp.float32),
            pltpu.VMEM((CORES, 8, count), jnp.float32),
            pltpu.VMEM((layers, 8, 128), jnp.float32),
            pltpu.VMEM((layers * CORES, 8, 128), jnp.float32),
            dma,
            dma((len(SIZES), 2)),
            dma((2,)),
            dma((2,)),
            dma((2,)),
            dma((len(SENDS),)),
            dma((len(SENDS),)),
            dma,
            dma,
            dma((layers * CORES,)),
            dma((layers * CORES,)),
            *(pltpu.VMEM((queries, 2, rank, UNIT * size), jnp.bfloat16) for size in SIZES),
        ],
        compiler_params=pltpu.CompilerParams(
            collective_id=0, has_side_effects=True, vmem_limit_bytes=55200 * 1024
        ),
        cost_estimate=pl.CostEstimate(flops=flops, bytes_accessed=12 * 2**20, transcendentals=0),
        name="gather_scores",
    )(doc_lengths, activations, backprops, out_factors, in_factors)
    return scores * scaling


def solution(mesh):
    placed = (
        P("layer", "dp", None),
        P("layer", "dp", None),
        P("layer", "dp", None, None),
        P("layer", "dp", None, None),
        P("dp", None),
    )
    return jax.shard_map(
        local, mesh=mesh, in_specs=placed, out_specs=P("layer", "dp"), check_vma=False
    )
```

```python
import functools
import math

import jax
import jax.numpy as jnp
from jax import lax
from jax.experimental import pallas as pl
from jax.experimental.pallas import tpu as pltpu
from jax.sharding import PartitionSpec as P

MESH = pl.DeviceIdType.MESH
RING = 8
LINES = 2
CORES = 2
SHARE = 6
UNIT = 128
SIZES = (18, 14, 8)

ORDER = (
    (0, 0, 0, 2), (0, 0, 0, 0), (1, 0, 0, 1), (-1, 0, 0, 1), (1, 0, 0, 2), (1, 0, 0, 0),
    (-1, 0, 0, 0), (-1, 0, 1, 1), (0, 0, -1, 1), (0, 0, 1, 1), (1, 0, -1, 2), (-1, 0, 1, 0),
    (0, 0, 0, 1), (1, 0, -1, 0), (1, 0, -1, 1), (-1, 0, 0, 2), (0, 0, 2, 1), (-1, 0, 2, 1),
    (0, 0, 2, 0), (1, 0, -2, 0), (-1, 0, 1, 2), (1, 0, -2, 1), (-1, 1, 2, 1), (1, 0, -2, 2),
    (0, 0, -2, 1), (0, 0, -2, 0), (0, 0, -3, 0), (-1, 0, 2, 2), (-1, 0, 2, 0), (1, 1, 0, 0),
    (1, 0, -3, 2), (1, 0, -3, 1), (-1, 0, 3, 1), (-1, 0, 3, 2), (-1, 1, 3, 1), (-1, 0, 3, 0),
    (0, 0, 3, 0), (1, 1, -2, 1), (2, 0, 0, 1), (1, 0, -3, 0), (0, 0, 3, 2), (1, 1, -3, 0),
    (0, 0, -3, 2), (-1, 1, 0, 0), (2, 0, 1, 0), (0, 0, 2, 2), (1, 1, 0, 2), (2, 0, 0, 2),
    (-1, 1, 3, 0), (2, 0, 1, 1), (0, 0, -2, 2), (2, 1, 1, 1), (2, 0, 1, 2), (-1, 1, 0, 2),
    (-1, 1, 3, 2), (1, 1, -3, 1), (2, 1, 0, 0), (1, 1, -3, 2), (2, 0, 0, 0), (2, 1, 1, 0),
    (2, 1, 0, 1), (2, 1, 0, 2), (2, 1, 1, 2),
)
SENDS = tuple(item for item in ORDER if item[0] != 2)
INDEX = {item: i for i, item in enumerate(SENDS)}


def far(offset):
    return RING // 2 if abs(offset) == RING // 2 else offset


def halves(item):
    way, _, offset, _ = item
    if way and abs(offset - way) == RING // 2:
        return (0,) if way == 1 else (1,)
    return (0, 1)


def arrival(item):
    way, line, offset, _ = item
    return (1 - line, far(offset)) if way == 0 else (line, far(offset - way))


ARRIVES = {(*arrival(item), half, item[3]): item for item in SENDS for half in halves(item)}


def kernel(
    layers, lens_ref, acts_ref, grads_ref, outs_ref, ins_ref, result_ref,
    lens, shown, tokens, proj, member, tiles, landed,
    lens_sem, own_sem, tok_sem, tok_send, tok_recv, send_sem, recv_sem, mem_send, mem_recv, tile_send, tile_recv,
    *gathered,
):
    dp, layer = lax.axis_index("dp"), lax.axis_index("layer")
    line, ring, core = dp // (RING * CORES), (dp // CORES) % RING, dp % CORES
    rank, width = outs_ref.shape[2], outs_ref.shape[3]
    count = acts_ref.shape[1]
    docs = lens_ref.shape[1]
    starts = [UNIT * sum(SIZES[:c]) for c in range(len(SIZES))]
    columns = [pl.ds(start, UNIT * size) for start, size in zip(starts, SIZES)]

    def device(line_, ring_, core_):
        return (line_ * RING + ring_) * CORES + core_

    up = (device(line, (ring + 1) % RING, core), layer)
    down = (device(line, (ring + RING - 1) % RING, core), layer)
    across = (device(1 - line, ring, core), layer)
    sibling = (device(line, ring, 1 - core), layer)
    hop = {1: up, -1: down, 0: across}

    barrier = pltpu.get_barrier_semaphore()
    for target in (up, down, across):
        pl.semaphore_signal(barrier, inc=1, device_id=target, device_id_type=MESH)

    mine = line * RING + ring
    half = pl.multiple_of(core * count, count)
    own = [
        pltpu.make_async_copy(f.at[0, 0, :, columns[c]], gathered[c].at[mine, i], own_sem.at[c, i])
        for c in range(len(SIZES))
        for i, f in enumerate((outs_ref, ins_ref))
    ]
    here = [
        pltpu.make_async_copy(t.at[0], tokens.at[i, pl.ds(half, count)], tok_sem.at[i])
        for i, t in enumerate((grads_ref, acts_ref))
    ]
    for copy in own[:2]:
        copy.start()
    for step in range(1, layers * CORES):
        to = (layer * CORES + core + step) % (layers * CORES)
        pl.semaphore_signal(
            barrier, inc=1, device_id=(device(line, ring, to % CORES), to // CORES), device_id_type=MESH
        )

    lengths = pltpu.make_async_copy(lens_ref, lens, lens_sem)
    lengths.start()
    for copy in own[2:]:
        copy.start()
    tiles[...] = jnp.zeros_like(tiles)
    for copy in own[:2]:
        copy.wait()
    pl.semaphore_wait(barrier, 3 + layers * CORES - 1)

    def block(line_, offset, item):
        part = halves(item)
        slot = (line if line_ == 0 else 1 - line) * RING + (ring + offset + RING) % RING
        return gathered[item[3]].at[slot, pl.ds(part[0], len(part))]

    def transfer(item, ref):
        i = INDEX[item]
        return pltpu.make_async_remote_copy(
            src_ref=ref, dst_ref=ref, send_sem=send_sem.at[i], recv_sem=recv_sem.at[i],
            device_id=hop[item[0]], device_id_type=MESH,
        )

    arrived = set()

    def need(line_, offset, half, c):
        item = ARRIVES.get((line_, far(offset), half, c))
        if item is not None and item not in arrived:
            arrived.add(item)
            transfer(item, block(*arrival(item), item)).wait_recv()

    shared = [
        pltpu.make_async_remote_copy(
            src_ref=t.at[0], dst_ref=tokens.at[i, pl.ds(half, count)],
            send_sem=tok_send.at[i], recv_sem=tok_recv.at[i], device_id=sibling, device_id_type=MESH,
        )
        for i, t in enumerate((grads_ref, acts_ref))
    ]
    theirs = pltpu.make_async_remote_copy(
        src_ref=member.at[core], dst_ref=member.at[core],
        send_sem=mem_send, recv_sem=mem_recv, device_id=sibling, device_id_type=MESH,
    )

    def multiply(line_, half, c, first, last):
        rows = (line if line_ == 0 else 1 - line) * RING
        left = gathered[c][pl.ds(rows, RING), half].reshape(RING * rank, UNIT * SIZES[c])
        into = pl.ds(pl.multiple_of(rows * rank, RING * rank), RING * rank)

        if last:
            terms = []
            for t in range(CORES):
                some = pl.ds(t * count, count)
                part = lax.dot_general(
                    left, tokens[half, some, columns[c]], (((1,), (1,)), ((), ())),
                    preferred_element_type=jnp.float32,
                )
                both = (proj[half, into, some] + part) * proj[1 - half, into, some]
                terms.append(both.reshape(RING, rank, count).sum(axis=1))
            return terms

        def tile(t, carry):
            some = pl.ds(pl.multiple_of(t * count, count), count)
            part = lax.dot_general(
                left, tokens[half, some, columns[c]], (((1,), (1,)), ((), ())),
                preferred_element_type=jnp.float32,
            )
            if first:
                proj[half, into, some] = part
            else:
                proj[half, into, some] += part
            return carry

        lax.fori_loop(0, CORES, tile, 0, unroll=c == len(SIZES) - 1)

    me, everyone = layer * CORES + core, layers * CORES
    each = LINES * RING // layers
    targets = RING // each

    def give(to, sender):
        return pltpu.make_async_remote_copy(
            src_ref=tiles.at[to // CORES], dst_ref=landed.at[sender],
            send_sem=tile_send.at[to], recv_sem=tile_recv.at[sender],
            device_id=(device(line, ring, to % CORES), to // CORES), device_id_type=MESH,
        )

    def finish(line_, first, terms):
        if first:
            pltpu.make_async_remote_copy(
                src_ref=member.at[1 - core], dst_ref=member.at[1 - core],
                send_sem=mem_send, recv_sem=mem_recv, device_id=sibling, device_id_type=MESH,
            ).wait_recv()
        which = line if line_ == 0 else 1 - line
        lane = lax.broadcasted_iota(jnp.int32, (RING, tiles.shape[2]), 1)
        scores = jnp.zeros(lane.shape, jnp.float32)
        for d in range(CORES * docs):
            t = d // docs
            mine_of = terms[t] * member[t, d : d + 1]
            scores = jnp.where(lane == d, mine_of.sum(axis=1, keepdims=True), scores)
        by_target = scores.reshape(targets, each, lane.shape[1])
        for i in range(each):
            for p in range(CORES):
                tiles[pl.ds(which * targets, targets), CORES * i + p, :] = jnp.where(core == p, by_target[:, i], 0.0)
        for k in range(targets * CORES):
            to = which * targets * CORES + k

            @pl.when(to != me)
            def _():
                give(to, me).start()

    def members():
        lengths.wait()
        position = lax.broadcasted_iota(jnp.int32, (8, count), 1)
        row = lax.broadcasted_iota(jnp.int32, (8, count), 0)
        held = jnp.zeros((8, count), jnp.float32)
        first = jnp.int32(0)
        for d in range(docs):
            after = first + lens[0, d]
            inside = (row == core * docs + d) & (position >= first) & (position < after)
            held = jnp.where(inside, 1.0, held)
            first = after
        member[core] = held

    other = pl.ds(pl.multiple_of((1 - core) * count, count), count)
    finished = []
    begun, counted, loaded = set(), {}, {0}
    for k, item in enumerate(ORDER):
        if k == SHARE:
            for copy in here + shared:
                copy.start()
            members()
            theirs.start()
        if item[0] != 2:
            if item[3] not in loaded and item[1:3] == (0, 0):
                loaded.add(item[3])
                for copy in own[2 * item[3] : 2 * item[3] + 2]:
                    copy.wait()
            for half in halves(item):
                need(item[1], item[2], half, item[3])
            transfer(item, block(item[1], item[2], item)).start()
            continue
        _, line_, half, c = item
        if half not in begun:
            begun.add(half)
            here[half].wait()
            pltpu.make_async_remote_copy(
                src_ref=(grads_ref, acts_ref)[half].at[0], dst_ref=tokens.at[half, other],
                send_sem=tok_send.at[half], recv_sem=tok_recv.at[half], device_id=sibling, device_id_type=MESH,
            ).wait_recv()
        for offset in range(RING):
            need(line_, offset if offset <= RING // 2 else offset - RING, half, c)
        first = (line_, half) not in counted.values()
        counted[item] = (line_, half)
        last = sum(way[0] == line_ for way in counted.values()) == 2 * len(SIZES)
        terms = multiply(line_, half, c, first, last)
        if last:
            finish(line_, len(finished) == 0, terms)
            finished.append(line_)

    for item in SENDS:
        transfer(item, block(item[1], item[2], item)).wait_send()
    for copy in shared:
        copy.wait_send()
    theirs.wait_send()
    total = tiles[layer]
    for step in range(1, everyone):
        give((me + step) % everyone, (me + step) % everyone).wait_recv()
        total = total + landed[(me + step) % everyone]
    for step in range(1, everyone):
        give((me + step) % everyone, me).wait_send()
    rows = total[0 : CORES * each]
    shown[...] = jnp.where(core == 0, rows[:, 0:docs], rows[:, docs : 2 * docs])
    answer = pltpu.make_async_copy(shown, result_ref, lens_sem)
    answer.start()
    answer.wait()


def local(activations, backprops, out_factors, in_factors, doc_lengths):
    count, width = activations.shape[1:]
    rank = out_factors.shape[2]
    docs = doc_lengths.shape[1]
    layers = lax.axis_size("layer") * activations.shape[0]
    queries = LINES * RING
    scaling = 1.0 / math.sqrt(rank * layers * count / docs)
    hbm = pl.BlockSpec(memory_space=pl.ANY)
    dma = pltpu.SemaphoreType.DMA
    flops = 2 * 2 * queries * rank * CORES * count * width
    scores = pl.pallas_call(
        functools.partial(kernel, layers),
        out_shape=jax.ShapeDtypeStruct((CORES * queries // layers, docs), jnp.float32),
        in_specs=[hbm] * 5,
        out_specs=hbm,
        scratch_shapes=[
            pltpu.SMEM((1, docs), jnp.int32),
            pltpu.VMEM((CORES * queries // layers, docs), jnp.float32),
            pltpu.VMEM((2, CORES * count, width), jnp.bfloat16),
            pltpu.VMEM((2, queries * rank, CORES * count), jnp.float32),
            pltpu.VMEM((CORES, 8, count), jnp.float32),
            pltpu.VMEM((layers, 8, 128), jnp.float32),
            pltpu.VMEM((layers * CORES, 8, 128), jnp.float32),
            dma,
            dma((len(SIZES), 2)),
            dma((2,)),
            dma((2,)),
            dma((2,)),
            dma((len(SENDS),)),
            dma((len(SENDS),)),
            dma,
            dma,
            dma((layers * CORES,)),
            dma((layers * CORES,)),
            *(pltpu.VMEM((queries, 2, rank, UNIT * size), jnp.bfloat16) for size in SIZES),
        ],
        compiler_params=pltpu.CompilerParams(
            collective_id=0, has_side_effects=True, vmem_limit_bytes=55200 * 1024
        ),
        cost_estimate=pl.CostEstimate(flops=flops, bytes_accessed=12 * 2**20, transcendentals=0),
        name="gather_scores",
    )(doc_lengths, activations, backprops, out_factors, in_factors)
    return scores * scaling


def solution(mesh):
    placed = (
        P("layer", "dp", None),
        P("layer", "dp", None),
        P("layer", "dp", None, None),
        P("layer", "dp", None, None),
        P("dp", None),
    )
    return jax.shard_map(
        local, mesh=mesh, in_specs=placed, out_specs=P("layer", "dp"), check_vma=False
    )
```

```python
import functools
import math

import jax
import jax.numpy as jnp
from jax import lax
from jax.experimental import pallas as pl
from jax.experimental.pallas import tpu as pltpu
from jax.sharding import PartitionSpec as P

MESH = pl.DeviceIdType.MESH
RING = 8
LINES = 2
CORES = 2
SHARE = 6
UNIT = 128
SIZES = (18, 14, 8)

ORDER = (
    (0, 0, 0, 2), (0, 0, 0, 0), (1, 0, 0, 1), (-1, 0, 0, 1), (1, 0, 0, 2), (1, 0, 0, 0),
    (-1, 0, 0, 0), (-1, 0, 1, 1), (0, 0, -1, 1), (0, 0, 1, 1), (1, 0, -1, 2), (-1, 0, 1, 0),
    (0, 0, 0, 1), (1, 0, -1, 0), (1, 0, -1, 1), (-1, 0, 0, 2), (0, 0, 2, 1), (-1, 0, 2, 1),
    (0, 0, 2, 0), (1, 0, -2, 0), (-1, 0, 1, 2), (1, 0, -2, 1), (-1, 1, 2, 1), (1, 0, -2, 2),
    (0, 0, -2, 1), (0, 0, -2, 0), (0, 0, -3, 0), (-1, 0, 2, 2), (-1, 0, 2, 0), (1, 1, 0, 0),
    (1, 0, -3, 2), (1, 0, -3, 1), (-1, 0, 3, 1), (-1, 0, 3, 2), (-1, 1, 3, 1), (-1, 0, 3, 0),
    (0, 0, 3, 0), (1, 1, -2, 1), (2, 0, 0, 1), (1, 0, -3, 0), (0, 0, 3, 2), (1, 1, -3, 0),
    (0, 0, -3, 2), (-1, 1, 0, 0), (2, 0, 1, 0), (0, 0, 2, 2), (1, 1, 0, 2), (2, 0, 0, 2),
    (-1, 1, 3, 0), (2, 0, 1, 1), (0, 0, -2, 2), (2, 1, 1, 1), (2, 0, 1, 2), (-1, 1, 0, 2),
    (-1, 1, 3, 2), (1, 1, -3, 1), (2, 1, 0, 0), (1, 1, -3, 2), (2, 0, 0, 0), (2, 1, 1, 0),
    (2, 1, 0, 1), (2, 1, 0, 2), (2, 1, 1, 2),
)
SENDS = tuple(item for item in ORDER if item[0] != 2)
INDEX = {item: i for i, item in enumerate(SENDS)}


def far(offset):
    return RING // 2 if abs(offset) == RING // 2 else offset


def halves(item):
    way, _, offset, _ = item
    if way and abs(offset - way) == RING // 2:
        return (0,) if way == 1 else (1,)
    return (0, 1)


def arrival(item):
    way, line, offset, _ = item
    return (1 - line, far(offset)) if way == 0 else (line, far(offset - way))


ARRIVES = {(*arrival(item), half, item[3]): item for item in SENDS for half in halves(item)}


def kernel(
    layers, lens_ref, acts_ref, grads_ref, outs_ref, ins_ref, result_ref,
    lens, shown, tokens, proj, member, tiles, landed,
    lens_sem, own_sem, tok_sem, tok_send, tok_recv, send_sem, recv_sem, mem_send, mem_recv, tile_send, tile_recv,
    *gathered,
):
    dp, layer = lax.axis_index("dp"), lax.axis_index("layer")
    line, ring, core = dp // (RING * CORES), (dp // CORES) % RING, dp % CORES
    rank, width = outs_ref.shape[2], outs_ref.shape[3]
    count = acts_ref.shape[1]
    docs = lens_ref.shape[1]
    starts = [UNIT * sum(SIZES[:c]) for c in range(len(SIZES))]
    columns = [pl.ds(start, UNIT * size) for start, size in zip(starts, SIZES)]

    def device(line_, ring_, core_):
        return (line_ * RING + ring_) * CORES + core_

    up = (device(line, (ring + 1) % RING, core), layer)
    down = (device(line, (ring + RING - 1) % RING, core), layer)
    across = (device(1 - line, ring, core), layer)
    sibling = (device(line, ring, 1 - core), layer)
    hop = {1: up, -1: down, 0: across}

    barrier = pltpu.get_barrier_semaphore()
    for target in (up, down, across):
        pl.semaphore_signal(barrier, inc=1, device_id=target, device_id_type=MESH)

    mine = line * RING + ring
    half = pl.multiple_of(core * count, count)
    own = [
        pltpu.make_async_copy(f.at[0, 0, :, columns[c]], gathered[c].at[mine, i], own_sem.at[c, i])
        for c in range(len(SIZES))
        for i, f in enumerate((outs_ref, ins_ref))
    ]
    here = [
        pltpu.make_async_copy(t.at[0], tokens.at[i, pl.ds(half, count)], tok_sem.at[i])
        for i, t in enumerate((grads_ref, acts_ref))
    ]
    for step in range(1, layers * CORES):
        to = (layer * CORES + core + step) % (layers * CORES)
        pl.semaphore_signal(
            barrier, inc=1, device_id=(device(line, ring, to % CORES), to // CORES), device_id_type=MESH
        )

    for copy in own[:2]:
        copy.start()
    lengths = pltpu.make_async_copy(lens_ref, lens, lens_sem)
    lengths.start()
    for copy in own[2:]:
        copy.start()
    tiles[...] = jnp.zeros_like(tiles)
    for copy in own[:2]:
        copy.wait()
    pl.semaphore_wait(barrier, 3 + layers * CORES - 1)

    def block(line_, offset, item):
        part = halves(item)
        slot = (line if line_ == 0 else 1 - line) * RING + (ring + offset + RING) % RING
        return gathered[item[3]].at[slot, pl.ds(part[0], len(part))]

    def transfer(item, ref):
        i = INDEX[item]
        return pltpu.make_async_remote_copy(
            src_ref=ref, dst_ref=ref, send_sem=send_sem.at[i], recv_sem=recv_sem.at[i],
            device_id=hop[item[0]], device_id_type=MESH,
        )

    arrived = set()

    def need(line_, offset, half, c):
        item = ARRIVES.get((line_, far(offset), half, c))
        if item is not None and item not in arrived:
            arrived.add(item)
            transfer(item, block(*arrival(item), item)).wait_recv()

    shared = [
        pltpu.make_async_remote_copy(
            src_ref=t.at[0], dst_ref=tokens.at[i, pl.ds(half, count)],
            send_sem=tok_send.at[i], recv_sem=tok_recv.at[i], device_id=sibling, device_id_type=MESH,
        )
        for i, t in enumerate((grads_ref, acts_ref))
    ]
    theirs = pltpu.make_async_remote_copy(
        src_ref=member.at[core], dst_ref=member.at[core],
        send_sem=mem_send, recv_sem=mem_recv, device_id=sibling, device_id_type=MESH,
    )

    def multiply(line_, half, c, first, last):
        rows = (line if line_ == 0 else 1 - line) * RING
        left = gathered[c][pl.ds(rows, RING), half].reshape(RING * rank, UNIT * SIZES[c])
        into = pl.ds(pl.multiple_of(rows * rank, RING * rank), RING * rank)

        if last:
            terms = []
            for t in range(CORES):
                some = pl.ds(t * count, count)
                part = lax.dot_general(
                    left, tokens[half, some, columns[c]], (((1,), (1,)), ((), ())),
                    preferred_element_type=jnp.float32,
                )
                both = (proj[half, into, some] + part) * proj[1 - half, into, some]
                terms.append(both.reshape(RING, rank, count).sum(axis=1))
            return terms

        def tile(t, carry):
            some = pl.ds(pl.multiple_of(t * count, count), count)
            part = lax.dot_general(
                left, tokens[half, some, columns[c]], (((1,), (1,)), ((), ())),
                preferred_element_type=jnp.float32,
            )
            if first:
                proj[half, into, some] = part
            else:
                proj[half, into, some] += part
            return carry

        lax.fori_loop(0, CORES, tile, 0, unroll=c == len(SIZES) - 1)

    me, everyone = layer * CORES + core, layers * CORES
    each = LINES * RING // layers
    targets = RING // each

    def give(to, sender):
        return pltpu.make_async_remote_copy(
            src_ref=tiles.at[to // CORES], dst_ref=landed.at[sender],
            send_sem=tile_send.at[to], recv_sem=tile_recv.at[sender],
            device_id=(device(line, ring, to % CORES), to // CORES), device_id_type=MESH,
        )

    def finish(line_, first, terms):
        if first:
            pltpu.make_async_remote_copy(
                src_ref=member.at[1 - core], dst_ref=member.at[1 - core],
                send_sem=mem_send, recv_sem=mem_recv, device_id=sibling, device_id_type=MESH,
            ).wait_recv()
        which = line if line_ == 0 else 1 - line
        lane = lax.broadcasted_iota(jnp.int32, (RING, tiles.shape[2]), 1)
        scores = jnp.zeros(lane.shape, jnp.float32)
        for d in range(CORES * docs):
            t = d // docs
            mine_of = terms[t] * member[t, d : d + 1]
            scores = jnp.where(lane == d, mine_of.sum(axis=1, keepdims=True), scores)
        by_target = scores.reshape(targets, each, lane.shape[1])
        for i in range(each):
            for p in range(CORES):
                tiles[pl.ds(which * targets, targets), CORES * i + p, :] = jnp.where(core == p, by_target[:, i], 0.0)
        for k in range(targets * CORES):
            to = which * targets * CORES + k

            @pl.when(to != me)
            def _():
                give(to, me).start()

    def members():
        lengths.wait()
        position = lax.broadcasted_iota(jnp.int32, (8, count), 1)
        row = lax.broadcasted_iota(jnp.int32, (8, count), 0)
        held = jnp.zeros((8, count), jnp.float32)
        first = jnp.int32(0)
        for d in range(docs):
            after = first + lens[0, d]
            inside = (row == core * docs + d) & (position >= first) & (position < after)
            held = jnp.where(inside, 1.0, held)
            first = after
        member[core] = held

    other = pl.ds(pl.multiple_of((1 - core) * count, count), count)
    finished = []
    begun, counted, loaded = set(), {}, {0}
    for k, item in enumerate(ORDER):
        if k == SHARE:
            for copy in here + shared:
                copy.start()
            members()
            theirs.start()
        if item[0] != 2:
            if item[3] not in loaded and item[1:3] == (0, 0):
                loaded.add(item[3])
                for copy in own[2 * item[3] : 2 * item[3] + 2]:
                    copy.wait()
            for half in halves(item):
                need(item[1], item[2], half, item[3])
            transfer(item, block(item[1], item[2], item)).start()
            continue
        _, line_, half, c = item
        if half not in begun:
            begun.add(half)
            here[half].wait()
            pltpu.make_async_remote_copy(
                src_ref=(grads_ref, acts_ref)[half].at[0], dst_ref=tokens.at[half, other],
                send_sem=tok_send.at[half], recv_sem=tok_recv.at[half], device_id=sibling, device_id_type=MESH,
            ).wait_recv()
        for offset in range(RING):
            need(line_, offset if offset <= RING // 2 else offset - RING, half, c)
        first = (line_, half) not in counted.values()
        counted[item] = (line_, half)
        last = sum(way[0] == line_ for way in counted.values()) == 2 * len(SIZES)
        terms = multiply(line_, half, c, first, last)
        if last:
            finish(line_, len(finished) == 0, terms)
            finished.append(line_)

    for item in SENDS:
        transfer(item, block(item[1], item[2], item)).wait_send()
    for copy in shared:
        copy.wait_send()
    theirs.wait_send()
    total = tiles[layer]
    for step in range(1, everyone):
        give((me + step) % everyone, (me + step) % everyone).wait_recv()
        total = total + landed[(me + step) % everyone]
    for step in range(1, everyone):
        give((me + step) % everyone, me).wait_send()
    rows = total[0 : CORES * each]
    shown[...] = jnp.where(core == 0, rows[:, 0:docs], rows[:, docs : 2 * docs])
    answer = pltpu.make_async_copy(shown, result_ref, lens_sem)
    answer.start()
    answer.wait()


def local(activations, backprops, out_factors, in_factors, doc_lengths):
    count, width = activations.shape[1:]
    rank = out_factors.shape[2]
    docs = doc_lengths.shape[1]
    layers = lax.axis_size("layer") * activations.shape[0]
    queries = LINES * RING
    scaling = 1.0 / math.sqrt(rank * layers * count / docs)
    hbm = pl.BlockSpec(memory_space=pl.ANY)
    dma = pltpu.SemaphoreType.DMA
    flops = 2 * 2 * queries * rank * CORES * count * width
    scores = pl.pallas_call(
        functools.partial(kernel, layers),
        out_shape=jax.ShapeDtypeStruct((CORES * queries // layers, docs), jnp.float32),
        in_specs=[hbm] * 5,
        out_specs=hbm,
        scratch_shapes=[
            pltpu.SMEM((1, docs), jnp.int32),
            pltpu.VMEM((CORES * queries // layers, docs), jnp.float32),
            pltpu.VMEM((2, CORES * count, width), jnp.bfloat16),
            pltpu.VMEM((2, queries * rank, CORES * count), jnp.float32),
            pltpu.VMEM((CORES, 8, count), jnp.float32),
            pltpu.VMEM((layers, 8, 128), jnp.float32),
            pltpu.VMEM((layers * CORES, 8, 128), jnp.float32),
            dma,
            dma((len(SIZES), 2)),
            dma((2,)),
            dma((2,)),
            dma((2,)),
            dma((len(SENDS),)),
            dma((len(SENDS),)),
            dma,
            dma,
            dma((layers * CORES,)),
            dma((layers * CORES,)),
            *(pltpu.VMEM((queries, 2, rank, UNIT * size), jnp.bfloat16) for size in SIZES),
        ],
        compiler_params=pltpu.CompilerParams(
            collective_id=0, has_side_effects=True, vmem_limit_bytes=55200 * 1024
        ),
        cost_estimate=pl.CostEstimate(flops=flops, bytes_accessed=12 * 2**20, transcendentals=0),
        name="gather_scores",
    )(doc_lengths, activations, backprops, out_factors, in_factors)
    return scores * scaling


def solution(mesh):
    placed = (
        P("layer", "dp", None),
        P("layer", "dp", None),
        P("layer", "dp", None, None),
        P("layer", "dp", None, None),
        P("dp", None),
    )
    return jax.shard_map(
        local, mesh=mesh, in_specs=placed, out_specs=P("layer", "dp"), check_vma=False
    )
```
